32 devices in a mesh: exp: 8 (over y, x, core), dp: 4 (over z).
Axes of the slice: x: 2, y: 2, z: 4, core: 2. Of those that a mesh axis runs over, the one named last changes fastest.
Arguments:
- hidden_in: bfloat16 [4096, 768], P(('exp', 'dp')), may hold values from -6 to 6
- cotangent: bfloat16 [4096, 768], P(('exp', 'dp')), may hold values from -6 to 6
- lengths: int32 [32, 3], P(('exp', 'dp')), may hold values from 1 to 96, 128 in all within a row
- routes: int32 [4096, 1], P(('exp', 'dp')), may hold values from 0 to 15; in each aligned block of 128 rows (0 to 127, 128 to 255, ...) at most 10 rows name the same one
- gain_attn: float32 [768], replicated, may hold values from 0.5 to 1.5
- attn_qkv: bfloat16 [768, 2304], P(('exp', 'dp')), may hold values from -0.21875 to 0.21875
- attn_out: bfloat16 [768, 768], P(('exp', 'dp')), may hold values from -0.875 to 0.875
- rel_bias: float32 [32, 12], replicated, may hold values from -3 to 3
- gain_ffn: float32 [768], replicated, may hold values from 0.5 to 1.5
- router: bfloat16 [768, 16], P(('exp', 'dp')), may hold values from -0.109375 to 0.109375
- expert_in: bfloat16 [16, 768, 3072], P('exp', None, 'dp'), may hold values from -0.21875 to 0.21875
- expert_out: bfloat16 [16, 3072, 768], P('exp', 'dp'), may hold values from -2.875 to 2.875
Outputs:
- mixed: bfloat16 [4096, 768], P(('exp', 'dp'))
- grad_in: float32 [4096, 768], P(('exp', 'dp'))
- grad_gain_attn: float32 [768], replicated
- grad_attn_qkv: float32 [768, 2304], P(('exp', 'dp'))
- grad_attn_out: float32 [768, 768], P(('exp', 'dp'))
- grad_rel_bias: float32 [32, 12], replicated
- grad_gain_ffn: float32 [768], replicated
- grad_router: float32 [768, 16], P(('exp', 'dp'))
- grad_expert_in: float32 [16, 768, 3072], P('exp', None, 'dp')
- grad_expert_out: float32 [16, 3072, 768], P('exp', 'dp')
The draws below stay inside these ranges and needn't reach their ends.
Inputs may be any that keep to these rules, and one draw needn't show every extreme that they name: `routes`: in the rows of one device no expert is named by more than 10 rows. The 3 lengths of one device sum to 128.
All inputs are finite; a program needn't handle non-finite values.
Results may differ from the reference program's by a relative error of at most 0.019.
Values may be sent and summed in bfloat16 or wider, within the bound.
A program may use at most 128 MiB of HBM per device.

```python
import math
import jax
import jax.numpy as jnp
import numpy as np
from jax import lax

D = 768
HEADS = 12
FF = 3072
BUCKETS = 32
TOK_DEV = 128
SEQ_DEV = 3
EXPERTS = 16
CAP = 10
MAX_LEN = 96
TOKENS = 4096
N_EXP = 8
N_DP = 4


def block_scale(rng, shape, pieces, low, top_value):
    gain, own = 1.0, jax.random.fold_in(rng, 6)
    for dim, blocks in pieces:
        heights = jnp.exp(jax.random.uniform(jax.random.fold_in(own, dim), (blocks,), jnp.float32, low / len(pieces), top_value / len(pieces)))
        gain = gain * jnp.repeat(heights, shape[dim] // blocks).reshape([-1 if axis == dim else 1 for axis in range(len(shape))])
    return gain


def profile(number_of, total, most, skew):
    weights = [(1 << 20) // math.isqrt(grade ** skew) + 1 for grade in range(2, number_of + 1)]
    spare, counts = total - most - (number_of - 1), [1] * (number_of - 1)
    while spare > 0:
        movable = [i for i in range(number_of - 1) if counts[i] < most]
        mass, budget = sum([weights[i] for i in movable]), spare
        for i in movable:
            addition = min(most - counts[i], max(1, budget * weights[i] // mass), spare)
            counts[i] = counts[i] + addition
            spare = spare - addition
    return np.array([most] + counts)


def ragged_sizes(key, amount, total, limit, skew):
    if amount == 2:
        one = jax.random.randint(key, (), max(1, total - limit), min(limit, total - 1) + 1)
        return jnp.stack([one, total - one])
    sizes = jnp.asarray(profile(amount, total, limit, skew), jnp.int32)
    pairs = (amount - 1) // 2
    source_of, receiver = sizes[1:1 + 2 * pairs:2], sizes[2:2 + 2 * pairs:2]
    slack = jnp.minimum(source_of - 1, limit - receiver)
    shifted = jax.random.randint(jax.random.fold_in(key, 1), (pairs,), 0, 1 << 20) % (slack + 1)
    sizes = sizes.at[1:1 + 2 * pairs:2].set(source_of - shifted).at[2:2 + 2 * pairs:2].set(receiver + shifted)
    return sizes[jax.random.permutation(jax.random.fold_in(key, 2), amount)]


def shared_out(key, own, number, rows, number_of, top, reach, slope):
    order = jax.random.permutation(key, number_of)
    crowded, ordinary = shares(number_of, rows * top, reach, slope, True), shares(number_of, rows * top, reach, slope, False)
    places = jnp.arange(number_of)

    def named(sizes, turn):
        used = int((sizes > 0).sum())
        fixed = max(1, used // 4)
        shifted = fixed + (places - fixed + turn * (used - fixed)) % max(1, number_of - fixed)
        return jnp.zeros((number_of,), jnp.int32).at[order[jnp.where(places < fixed, places, shifted)]].set(jnp.asarray(sizes, jnp.int32))

    sizes = jnp.where(number % 4 == 0, named(crowded, number // 4), named(ordinary, number - number // 4 - 1))
    mixed = jax.random.permutation(jax.random.fold_in(own, 3), number_of)
    source_of, receiver = mixed[0:number_of // 2 * 2:2], mixed[1:number_of // 2 * 2:2]
    slack = jnp.minimum(sizes[source_of] - 1, reach - sizes[receiver]) // 2
    slack = jnp.where((source_of == order[0]) | (receiver == order[0]) | (sizes[receiver] == 0), 0, jnp.maximum(slack, 0))
    shifted = jax.random.randint(jax.random.fold_in(own, 4), (number_of // 2,), 0, 1 << 20) % (slack + 1)
    sizes = sizes.at[source_of].add(-shifted).at[receiver].add(shifted)
    members = jnp.searchsorted(jnp.cumsum(sizes), jnp.arange(rows * top), side="right").astype(jnp.int32)
    grid = members.reshape(top, rows).T
    grid = grid[jax.random.permutation(jax.random.fold_in(own, 1), rows)]
    turn = jax.random.randint(jax.random.fold_in(own, 2), (rows, 1), 0, top)
    return jnp.take_along_axis(grid, (jnp.arange(top)[None, :] + turn) % top, axis=1)


def shares(amount, total, bound, skew, full):
    weights = [(1 << 20) // math.isqrt(rank ** skew) + 1 for rank in range(1, amount + 1)]
    largest = bound if full else min(bound, max(-(-total // amount), total * weights[0] // sum(weights)))
    least = 1 if total - largest >= amount - 1 else 0
    holding, surplus = [largest] + [least] * (amount - 1), total - largest - least * (amount - 1)
    while surplus > 0:
        free = [i for i in range(1, amount) if holding[i] < largest] or [i for i in range(1, amount) if holding[i] < bound]
        mass, left = sum([weights[i] for i in free]), surplus
        for i in free:
            more = min(bound - holding[i], max(1, left * weights[i] // mass), surplus)
            holding[i] = holding[i] + more
            surplus = surplus - more
    return np.array(holding)


def gaussian(own_key, extent, width, limit, cuts=(), kind=jnp.bfloat16):
    result = jax.random.normal(own_key, extent, jnp.float32) * width
    if len(cuts) > 0:
        result = block_scale(own_key, extent, cuts, -0.22, 0.18) * result
    return jnp.clip(result, min=-limit, max=limit).astype(kind)


def setup_inputs(seed: int = 0) -> dict:
    splits = jax.random.split(jax.random.key(seed), 13)
    hidden_in = gaussian(splits[0], (TOKENS, D), 1.0, 6.0, ((0, 32),))
    cotangent = gaussian(splits[1], (TOKENS, D), 1.0, 6.0, ((0, 32),))
    lengths = jax.vmap(lambda own: ragged_sizes(own, SEQ_DEV, TOK_DEV, MAX_LEN, 2))(jax.random.split(splits[2], (N_EXP * N_DP))).reshape((N_EXP * N_DP, SEQ_DEV)).astype(jnp.int32)
    routes_keys = jax.random.split(jax.random.fold_in(splits[3], 1), TOKENS // TOK_DEV)
    routes_turns = jax.random.permutation(jax.random.fold_in(splits[3], 3), TOKENS // TOK_DEV)
    routes = jax.vmap(lambda own, number: shared_out(jax.random.fold_in(splits[3], 2), own, number, TOK_DEV, EXPERTS, 1, CAP, 1))(routes_keys, routes_turns).reshape((TOKENS, 1))
    gain_attn = jnp.clip(1.0 + 0.1 * jax.random.normal(splits[4], (D,), jnp.float32), 0.5, 1.5)
    attn_qkv = gaussian(splits[5], (D, 3 * D), D ** -0.5, 0.21875, ((0, 32),))
    attn_out = gaussian(splits[6], (D, D), (D // 16) ** -0.5, 0.875, ((0, 32),))
    rel_bias = gaussian(splits[7], (BUCKETS, HEADS), 0.5, 3.0, (), jnp.float32)
    gain_ffn = jnp.clip(1.0 + 0.1 * jax.random.normal(splits[8], (D,), jnp.float32), 0.5, 1.5)
    router = gaussian(splits[9], (D, EXPERTS), (4 * D) ** -0.5, 0.109375, ((0, 32),))
    expert_in = gaussian(splits[10], (EXPERTS, D, FF), D ** -0.5, 0.21875, ((0, 8), (2, 4)))
    expert_out = gaussian(splits[11], (EXPERTS, FF, D), (0.031 * EXPERTS), 2.875, ((0, 8), (1, 4)))
    return {"hidden_in": hidden_in, "cotangent": cotangent, "lengths": lengths, "routes": routes, "gain_attn": gain_attn, "attn_qkv": attn_qkv, "attn_out": attn_out, "rel_bias": rel_bias, "gain_ffn": gain_ffn, "router": router, "expert_in": expert_in, "expert_out": expert_out}


@jax.custom_vjp
def low(v):
    return lax.optimization_barrier(v.astype(jnp.bfloat16)).astype(jnp.float32)

@jax.custom_vjp
def low_back(v):
    return v

def low_keep(v):
    return (low(v), None)

def low_pass(kept, grad):
    return (grad,)

def back_keep(v):
    return (v, None)

def back_low(kept, grad):
    return (low(grad),)
low.defvjp(low_keep, low_pass)
low_back.defvjp(back_keep, back_low)
epsilon = 1e-06
highest = lax.Precision.HIGHEST

def bucket_table(row_count, bucket_count):
    offset = np.arange(row_count)[None, :] - np.arange(row_count)[:, None]
    half_count = bucket_count // 2
    exact_count = half_count // 2
    spread = np.abs(offset)
    scaled = np.log(np.maximum(spread, 1) / exact_count) / np.log(128.0 / exact_count) * (half_count - exact_count)
    distant = np.minimum(exact_count + np.maximum(scaled, 0.0).astype(np.int32), half_count - 1)
    return ((offset > 0) * half_count + np.where(spread < exact_count, spread, distant)).astype(np.int32)

def rms_norm(values, gain_vec):
    return values * lax.rsqrt(lax.optimization_barrier(jnp.mean(values * values, axis=-1, keepdims=True)) + epsilon) * gain_vec

def gelu_tanh(values):
    return jax.nn.gelu(values, approximate=True)

def segment_ids(lengths, row_count):
    boundary = jnp.cumsum(lengths, axis=-1).astype(jnp.int32)
    position = jnp.arange(row_count, dtype=jnp.int32)
    return lax.optimization_barrier(jnp.sum((position[:, None] >= boundary[..., None, :]).astype(jnp.int32), axis=-1)).astype(jnp.int32)

def attend_block(qkv_rows, segment, pos_bias):
    row_count = qkv_rows.shape[0]
    model_width = qkv_rows.shape[1] // 3
    head_count = pos_bias.shape[0]
    head_size = model_width // head_count
    queries = qkv_rows[:, :model_width].reshape(row_count, head_count, head_size)
    key_rows = qkv_rows[:, model_width:2 * model_width].reshape(row_count, head_count, head_size)
    value_rows = qkv_rows[:, 2 * model_width:].reshape(row_count, head_count, head_size)
    scores = jnp.einsum('qhe,khe->hqk', queries, key_rows, precision=highest) * head_size ** (-0.5) + pos_bias
    scores = low_back(scores)
    allowed = (segment[:, None] == segment[None, :])[None]
    scores = jnp.where(allowed, scores, -1e+30)
    attn_probs = jax.nn.softmax(scores, axis=-1)
    attended = jnp.einsum('hqk,khe->qhe', low(attn_probs), value_rows, precision=highest)
    return attended.reshape(row_count, model_width)

def expert_block(triple):
    slot_batch, weight_in, weight_out = triple
    hidden_pre = low_back(jnp.dot(slot_batch, weight_in, precision=highest))
    active = low(gelu_tanh(hidden_pre))
    return low_back(low(jnp.dot(active, weight_out, precision=highest)))

def reference(hidden_in, cotangent, lengths, routes, gain_attn, attn_qkv, attn_out, rel_bias, gain_ffn, router, expert_in, expert_out):
    device_count = N_EXP * N_DP
    segment = segment_ids(lengths, TOK_DEV)
    bucket_ids = bucket_table(TOK_DEV, BUCKETS)
    choose = (routes[:, 0:1] == jnp.arange(EXPERTS, dtype=jnp.int32)[None, :]).astype(jnp.int32)
    rank_index = jnp.cumsum(choose.reshape(device_count, TOK_DEV, EXPERTS), axis=1).astype(jnp.int32)
    rank_index = rank_index.reshape(TOKENS, EXPERTS) - 1
    slot_index = lax.optimization_barrier(jnp.sum(rank_index * choose, axis=1)).astype(jnp.int32)
    device_ids = (jnp.arange(TOKENS, dtype=jnp.int32) // TOK_DEV).astype(jnp.int32)
    slot_place = (routes[:, 0] * (device_count * CAP) + device_ids * CAP + slot_index).astype(jnp.int32)

    def layer(inputs, gain_one, qkv_weight, out_weight, bias_table, gain_two, route_weight, weight_in, weight_out):
        normed = low(rms_norm(inputs, gain_one))
        qkv_rows = low_back(low(jnp.dot(normed, qkv_weight, precision=highest)))
        pos_bias = jnp.transpose(bias_table[bucket_ids], (2, 0, 1))
        blocks = qkv_rows.reshape(device_count, TOK_DEV, 3 * D)

        def attend_one(block_pair):
            return attend_block(block_pair[0], block_pair[1], pos_bias)
        attended = lax.map(jax.checkpoint(attend_one), (blocks, segment)).reshape(TOKENS, D)
        attended = low_back(low(attended))
        middle = inputs + low_back(jnp.dot(attended, out_weight, precision=highest))
        ffn_in = low(rms_norm(middle, gain_two))
        logits = low_back(jnp.dot(ffn_in, route_weight, precision=highest))
        gate_probs = jax.nn.softmax(logits, axis=-1)
        gate_prob = jnp.take_along_axis(gate_probs, routes, axis=1)
        slot_rows = jnp.zeros((EXPERTS * device_count * CAP, D), jnp.float32).at[slot_place].set(ffn_in)
        slot_rows = slot_rows.reshape(EXPERTS, device_count * CAP, D)
        results = lax.map(jax.checkpoint(expert_block), (slot_rows, weight_in, weight_out)).reshape(EXPERTS * device_count * CAP, D)
        return middle + gate_prob * results[slot_place]
    mixed, layer_pull = jax.vjp(layer, hidden_in.astype(jnp.float32), gain_attn, attn_qkv.astype(jnp.float32), attn_out.astype(jnp.float32), rel_bias, gain_ffn, router.astype(jnp.float32), expert_in.astype(jnp.float32), expert_out.astype(jnp.float32))
    gradients = layer_pull(cotangent.astype(jnp.float32))
    return (mixed.astype(jnp.bfloat16), gradients[0], gradients[1], gradients[2], gradients[3], gradients[4], gradients[5], gradients[6], gradients[7], gradients[8])
```

```python
import functools

import jax
import jax.numpy as jnp
import numpy as np
from jax import lax
from jax.experimental import pallas as pl
from jax.experimental.pallas import tpu as pltpu
from jax.sharding import PartitionSpec as P

MESH = pl.DeviceIdType.MESH
lane_count = 128
by_y = (0, 3)

epsilon = 1e-06


def bucket_table(row_count, bucket_count):
    offset = np.arange(row_count)[None, :] - np.arange(row_count)[:, None]
    half_count = bucket_count // 2
    exact_count = half_count // 2
    spread = np.abs(offset)
    scaled = (
        np.log(np.maximum(spread, 1) / exact_count)
        / np.log(128.0 / exact_count)
        * (half_count - exact_count)
    )
    distant = np.minimum(exact_count + np.maximum(scaled, 0.0).astype(np.int32), half_count - 1)
    return ((offset > 0) * half_count + np.where(spread < exact_count, spread, distant)).astype(
        np.int32
    )


def rms_norm(values, gain_vec):
    return (
        values * lax.rsqrt(jnp.mean(values * values, axis=-1, keepdims=True) + epsilon) * gain_vec
    )


def gelu_tanh(values):
    return jax.nn.gelu(values, approximate=True)


def segment_ids(lengths, row_count):
    boundary = jnp.cumsum(lengths, axis=-1)
    position = jnp.arange(row_count, dtype=jnp.int32)
    return jnp.sum((position[:, None] >= boundary[..., None, :]).astype(jnp.int32), axis=-1)


def score_block(queries, key_rows, pos_bias, allowed, score_scale):
    scores = (
        jnp.einsum("qhe,khe->hqk", queries, key_rows, preferred_element_type=jnp.float32)
        * score_scale
        + pos_bias
    )
    return jnp.where(allowed, scores, -1e30)


def positions():
    e, z = lax.axis_index("exp"), lax.axis_index("dp")
    core, side_x, side_y = lax.rem(e, 2), lax.rem(lax.div(e, 2), 2), lax.div(e, 4)
    step_core, step_x, step_y = 1 - 2 * core, 2 - 4 * side_x, 4 - 8 * side_y
    chips = (e, e + step_x, e + step_y, e + step_x + step_y)
    return e, z, step_core, chips


def greet(devices):
    barrier = pltpu.get_barrier_semaphore()
    for device in devices:
        pl.semaphore_signal(barrier, inc=1, device_id=device, device_id_type=MESH)
    pl.semaphore_wait(barrier, len(devices))


def gather_kernel(mine_ref, full_ref, local_sem, send_sem, recv_sem):
    e, z, step_core, chips = positions()
    zs = [lax.rem(z + j, 4) for j in range(4)]
    partner = (e + step_core, z)
    beside = {1: (chips[1], z), 2: (chips[2], z)}
    along = {j: (e, zs[j]) for j in (1, 2, 3)}
    greet([partner, beside[1], beside[2], along[1], along[2], along[3]])
    sends = []

    def send(src, chip, j, device, recv):
        copy = pltpu.make_async_remote_copy(
            src_ref=src,
            dst_ref=full_ref.at[chips[chip] * 4 + zs[j]],
            send_sem=send_sem.at[len(sends)],
            recv_sem=recv_sem.at[recv],
            device_id=device,
            device_id_type=MESH,
        )
        copy.start()
        sends.append(copy)

    def held(chip, j):
        return full_ref.at[chips[chip] * 4 + zs[j]]

    def arrive(place, recv):
        pltpu.make_async_remote_copy(
            src_ref=place,
            dst_ref=place,
            send_sem=send_sem.at[0],
            recv_sem=recv_sem.at[recv],
            device_id=partner,
            device_id_type=MESH,
        ).wait_recv()

    def spread(src, j):
        send(src, 0, j, beside[1], 4 + j)
        send(src, 0, j, beside[2], 8 + j)
        send(src, 0, j, partner, 16 + j)

    def from_x(j):
        arrive(held(1, j), 4 + j)
        if j in by_y:
            send(held(1, j), 1, j, beside[2], 12 + j)
        send(held(1, j), 1, j, partner, 20 + j)

    def from_y(j):
        arrive(held(2, j), 8 + j)
        if j not in by_y:
            send(held(2, j), 2, j, beside[1], 12 + j)
        send(held(2, j), 2, j, partner, 24 + j)

    own = pltpu.make_async_copy(mine_ref, held(0, 0), local_sem)
    own.start()
    for j in (1, 3, 2):
        send(mine_ref, 0, 0, along[j], (4 - j) % 4)
    spread(mine_ref, 0)
    for j in (3, 1):
        arrive(held(0, j), j)
        spread(held(0, j), j)
    from_x(0)
    from_y(0)
    arrive(held(0, 2), 2)
    spread(held(0, 2), 2)
    for j in (3, 1, 2):
        from_x(j)
        from_y(j)
    for j in (0, 3, 1, 2):
        arrive(held(3, j), 12 + j)
        send(held(3, j), 3, j, partner, 28 + j)
    for chip in range(4):
        for j in range(4):
            arrive(full_ref.at[(chips[chip] + step_core) * 4 + zs[j]], 16 + chip * 4 + j)
    for copy in sends:
        copy.wait_send()
    own.wait()


def gather_rows(mine):
    rows, width = mine.shape
    full = pl.pallas_call(
        gather_kernel,
        out_shape=jax.ShapeDtypeStruct((32, rows, width), mine.dtype),
        in_specs=[pl.BlockSpec(memory_space=pl.ANY)],
        out_specs=pl.BlockSpec(memory_space=pl.ANY),
        scratch_shapes=[
            pltpu.SemaphoreType.DMA,
            pltpu.SemaphoreType.DMA((31,)),
            pltpu.SemaphoreType.DMA((32,)),
        ],
        compiler_params=pltpu.CompilerParams(collective_id=0, has_side_effects=True),
        cost_estimate=pl.CostEstimate(flops=0, bytes_accessed=64 * rows * width, transcendentals=0),
        name="gather_rows",
    )(mine)
    return full.reshape(32 * rows, width)


def reduce_kernel(
    grad_ref, small_ref, out_ref, total_ref,
    from_core, summed, passing, from_x, from_y, from_z,
    small_sum, small_in, small_z, send_sem, recv_sem, small_send, small_recv,
):
    e, z, step_core, chips = positions()
    zs = [lax.rem(z + j, 4) for j in range(4)]
    partner = (e + step_core, z)
    beside = {1: (chips[1], z), 2: (chips[2], z)}
    along = {j: (e, zs[j]) for j in (1, 2, 3)}
    greet([partner, beside[1], beside[2], along[1], along[2], along[3]])
    sends = []

    def send(src, dst, device, recv):
        copy = pltpu.make_async_remote_copy(
            src_ref=src,
            dst_ref=dst,
            send_sem=send_sem.at[len(sends)],
            recv_sem=recv_sem.at[recv],
            device_id=device,
            device_id_type=MESH,
        )
        copy.start()
        sends.append(copy)

    def small_copy(src, dst, device, number, recv):
        return pltpu.make_async_remote_copy(
            src_ref=src,
            dst_ref=dst,
            send_sem=small_send.at[number],
            recv_sem=small_recv.at[recv],
            device_id=device,
            device_id_type=MESH,
        )

    def arrive(place, recv):
        pltpu.make_async_remote_copy(
            src_ref=place,
            dst_ref=place,
            send_sem=send_sem.at[0],
            recv_sem=recv_sem.at[recv],
            device_id=partner,
            device_id_type=MESH,
        ).wait_recv()
        return place[...].astype(jnp.float32)

    def pair(chip, j):
        number = chip * 4 + j
        mine = grad_ref[chips[chip] * 4 + zs[j]].astype(jnp.float32)
        return mine + arrive(from_core.at[number], number)

    def step_sum(number, device):
        copy = small_copy(small_sum.at[number], small_in.at[number], device, number, number)
        copy.start()
        copy.wait_recv()
        small_sum[number + 1] = small_sum[number] + small_in[number]
        return copy

    small_sum[0] = small_ref[...]
    for chip in (3, 1, 2, 0):
        for j in (0, 1, 3, 2):
            place = (chips[chip] + step_core) * 4 + zs[j]
            send(grad_ref.at[place], from_core.at[chip * 4 + j], partner, chip * 4 + j)
    small_copies = [step_sum(0, partner)]
    for j in (0, 1, 3, 2):
        number = 12 + j
        summed[number] = pair(3, j).astype(jnp.bfloat16)
        device = beside[2] if j in by_y else beside[1]
        send(summed.at[number], passing.at[j], device, 16 + j)
    small_copies.append(step_sum(1, beside[1]))
    for j, chip in ((1, 1), (0, 2), (2, 1), (3, 2), (0, 1), (1, 2), (3, 1), (2, 2)):
        number = chip * 4 + j
        value = pair(chip, j)
        if (j in by_y) == (chip == 1):
            value = value + arrive(passing.at[j], 16 + j)
        summed[number] = value.astype(jnp.bfloat16)
        landing = from_x if chip == 1 else from_y
        send(summed.at[number], landing.at[j], beside[chip], 16 + number)
    small_copies.append(step_sum(2, beside[2]))
    small_z[0] = small_sum[3]
    for j in (1, 2, 3):
        copy = small_copy(small_z.at[0], small_z.at[4 - j], along[j], 2 + j, 6 - j)
        copy.start()
        small_copies.append(copy)
    for j in (1, 2, 3, 0):
        value = pair(0, j) + arrive(from_x.at[j], 20 + j) + arrive(from_y.at[j], 24 + j)
        if j == 0:
            for other in (1, 2, 3):
                value = value + arrive(from_z.at[other - 1], 27 + other)
            out_ref[...] = value
        else:
            summed[j] = value.astype(jnp.bfloat16)
            send(summed.at[j], from_z.at[3 - j], along[j], 31 - j)
    for copy in small_copies[3:]:
        copy.wait_recv()
    spot = [lax.rem(4 + k - z, 4) for k in range(4)]
    total_ref[...] = (small_z[spot[0]] + small_z[spot[1]]) + (small_z[spot[2]] + small_z[spot[3]])
    for copy in sends + small_copies:
        copy.wait_send()


def reduce_rows(grads, small):
    _, rows, width = grads.shape
    vmem = pl.BlockSpec(memory_space=pltpu.VMEM)
    block = functools.partial(pltpu.VMEM, dtype=jnp.bfloat16)
    return pl.pallas_call(
        reduce_kernel,
        out_shape=(
            jax.ShapeDtypeStruct((rows, width), jnp.float32),
            jax.ShapeDtypeStruct(small.shape, jnp.float32),
        ),
        in_specs=[vmem, vmem],
        out_specs=(vmem, vmem),
        scratch_shapes=[
            block((16, rows, width)),
            block((16, rows, width)),
            block((4, rows, width)),
            block((4, rows, width)),
            block((4, rows, width)),
            block((3, rows, width)),
            pltpu.VMEM((4,) + small.shape, jnp.float32),
            pltpu.VMEM((3,) + small.shape, jnp.float32),
            pltpu.VMEM((4,) + small.shape, jnp.float32),
            pltpu.SemaphoreType.DMA((31,)),
            pltpu.SemaphoreType.DMA((31,)),
            pltpu.SemaphoreType.DMA((6,)),
            pltpu.SemaphoreType.DMA((6,)),
        ],
        compiler_params=pltpu.CompilerParams(
            collective_id=1, has_side_effects=True, vmem_limit_bytes=40 * 1024 * 1024
        ),
        cost_estimate=pl.CostEstimate(
            flops=64 * rows * width, bytes_accessed=64 * rows * width, transcendentals=0
        ),
        name="reduce_rows",
    )(grads, small)


def local(
    hidden_in,
    cotangent,
    lengths,
    routes,
    gain_attn,
    attn_qkv,
    attn_out,
    rel_bias,
    gain_ffn,
    router,
    expert_in,
    expert_out,
):
    row_count, model_width = hidden_in.shape
    bucket_count, head_count = rel_bias.shape
    head_size = model_width // head_count
    score_scale = head_size ** (-0.5)
    expert_count = router.shape[1]
    group_count = lax.axis_size("exp")
    local_count = expert_in.shape[0]
    capacity = max(2, row_count * 5 // (4 * expert_count))
    dp_count = lax.axis_size("dp")
    shard_rows = attn_qkv.shape[0]
    direct = group_count == 8 and dp_count == 4 and shard_rows % 8 == 0
    dense_width = 4 * model_width + expert_count
    full_width = -(-dense_width // lane_count) * lane_count
    shard = jnp.concatenate(
        [
            attn_qkv,
            attn_out,
            router,
            jnp.zeros((shard_rows, full_width - dense_width), jnp.bfloat16),
        ],
        axis=1,
    )
    if direct:
        full = gather_rows(shard)
    else:
        full = lax.all_gather(shard, ("exp", "dp"), axis=0, tiled=True)
    full_qkv = full[:, : 3 * model_width]
    full_out = full[:, 3 * model_width : 4 * model_width]
    full_route = full[:, 4 * model_width : dense_width]
    inputs = hidden_in.astype(jnp.float32)
    normed, attn_norm_pull = jax.vjp(rms_norm, inputs, gain_attn)
    normed_low = normed.astype(jnp.bfloat16)
    qkv_low = jnp.dot(normed_low, full_qkv, preferred_element_type=jnp.float32).astype(jnp.bfloat16)
    queries = qkv_low[:, :model_width].reshape(row_count, head_count, head_size)
    key_rows = qkv_low[:, model_width : 2 * model_width].reshape(row_count, head_count, head_size)
    value_rows = qkv_low[:, 2 * model_width :].reshape(row_count, head_count, head_size)
    bucket_ids = bucket_table(row_count, bucket_count)
    bucket_hot = jnp.asarray(
        bucket_ids.reshape(1, -1) == np.arange(bucket_count)[:, None], dtype=jnp.bfloat16
    )
    pos_bias = jnp.einsum(
        "bh,bn->hn",
        rel_bias,
        bucket_hot.astype(jnp.float32),
        precision=lax.Precision.HIGHEST,
    ).reshape(head_count, row_count, row_count)
    segment = segment_ids(lengths, row_count)[0]
    allowed = (segment[:, None] == segment[None, :])[None]
    scores = score_block(queries, key_rows, pos_bias, allowed, score_scale)
    row_max = jnp.max(scores, axis=-1, keepdims=True)
    log_total = row_max + jnp.log(jnp.sum(jnp.exp(scores - row_max), axis=-1, keepdims=True))
    attn_probs = jnp.exp(scores - log_total)
    attended = jnp.einsum(
        "hqk,khe->qhe",
        attn_probs.astype(jnp.bfloat16),
        value_rows,
        preferred_element_type=jnp.float32,
    )
    attended_low = attended.reshape(row_count, model_width).astype(jnp.bfloat16)
    middle = inputs + jnp.dot(attended_low, full_out, preferred_element_type=jnp.float32)
    ffn_norm, ffn_norm_pull = jax.vjp(rms_norm, middle, gain_ffn)
    ffn_low = ffn_norm.astype(jnp.bfloat16)
    gate_probs = jax.nn.softmax(
        jnp.dot(ffn_low, full_route, preferred_element_type=jnp.float32), axis=-1
    )
    choose = routes == jnp.arange(expert_count, dtype=jnp.int32)[None, :]
    gate_prob = jnp.sum(jnp.where(choose, gate_probs, 0.0), axis=1, keepdims=True)
    rank_index = jnp.cumsum(choose.astype(jnp.int32), axis=0) - 1
    slot_index = jnp.sum(jnp.where(choose, rank_index, 0), axis=1)
    slot_place = routes[:, 0] * capacity + slot_index
    dispatch = (
        jnp.arange(expert_count * capacity, dtype=jnp.int32)[:, None] == slot_place[None, :]
    ).astype(jnp.bfloat16)
    grad_out = cotangent.astype(jnp.float32)
    grad_picked = (gate_prob * grad_out).astype(jnp.bfloat16)
    outgoing = jnp.dot(
        dispatch,
        jnp.concatenate([ffn_low, grad_picked], axis=1),
        preferred_element_type=jnp.float32,
    ).astype(jnp.bfloat16)
    outgoing = outgoing.reshape(group_count, local_count, capacity, 2 * model_width)
    arrived = lax.all_to_all(outgoing, "exp", split_axis=0, concat_axis=0, tiled=True)
    gathered = lax.all_gather(arrived[None], "dp", axis=0, tiled=True)
    slot_rows = dp_count * group_count * capacity
    gathered = jnp.transpose(gathered, (2, 0, 1, 3, 4)).reshape(
        local_count, slot_rows, 2 * model_width
    )
    expert_rows = gathered[:, :, :model_width]
    grad_result = gathered[:, :, model_width:]
    hidden_pre = jnp.einsum(
        "lsd,ldf->lsf", expert_rows, expert_in, preferred_element_type=jnp.float32
    )
    active_f32, gelu_pull = jax.vjp(gelu_tanh, hidden_pre)
    active = active_f32.astype(jnp.bfloat16)
    partial_out = jnp.einsum("lsf,lfd->lsd", active, expert_out, preferred_element_type=jnp.float32)
    grad_active = jnp.einsum(
        "lsd,lfd->lsf", grad_result, expert_out, preferred_element_type=jnp.float32
    )
    grad_pre = gelu_pull(grad_active)[0].astype(jnp.bfloat16)
    grad_part = jnp.einsum("lsf,ldf->lsd", grad_pre, expert_in, preferred_element_type=jnp.float32)
    grad_expert_out = jnp.einsum(
        "lsf,lsd->lfd", active, grad_result, preferred_element_type=jnp.float32
    )
    grad_expert_in = jnp.einsum(
        "lsd,lsf->ldf", expert_rows, grad_pre, preferred_element_type=jnp.float32
    )
    partial = jnp.concatenate(
        [partial_out.astype(jnp.bfloat16), grad_part.astype(jnp.bfloat16)], axis=2
    ).reshape(local_count, dp_count, group_count, capacity, 2 * model_width)
    partial = jnp.transpose(partial, (1, 2, 0, 3, 4))
    result_rows = lax.psum_scatter(partial, "dp", scatter_dimension=0, tiled=True)[0]
    returned = lax.all_to_all(result_rows, "exp", split_axis=0, concat_axis=0, tiled=True)
    picked_both = lax.dot_general(
        dispatch,
        returned.reshape(expert_count * capacity, 2 * model_width),
        (((0,), (0,)), ((), ())),
        preferred_element_type=jnp.float32,
    )
    picked = picked_both[:, :model_width]
    grad_ffn = picked_both[:, model_width:]
    mixed = (middle + gate_prob * picked).astype(jnp.bfloat16)
    gate_grad = jnp.sum(grad_out * picked, axis=1, keepdims=True)
    logit_grad = (gate_probs * (jnp.where(choose, gate_grad, 0.0) - gate_prob * gate_grad)).astype(
        jnp.bfloat16
    )
    grad_ffn = grad_ffn + jnp.dot(logit_grad, full_route.T, preferred_element_type=jnp.float32)
    grad_router = jnp.einsum("td,te->de", ffn_low, logit_grad, preferred_element_type=jnp.float32)
    grad_middle_norm, grad_gain_ffn = ffn_norm_pull(grad_ffn)
    grad_middle = grad_out + grad_middle_norm
    branch_grad = grad_middle.astype(jnp.bfloat16)
    grad_attn_out = jnp.einsum(
        "td,te->de", attended_low, branch_grad, preferred_element_type=jnp.float32
    )
    grad_attended = jnp.dot(branch_grad, full_out.T, preferred_element_type=jnp.float32).astype(
        jnp.bfloat16
    )
    grad_attended = grad_attended.reshape(row_count, head_count, head_size)
    scores = score_block(queries, key_rows, pos_bias, allowed, score_scale)
    attn_probs = jnp.exp(scores - log_total)
    grad_values = jnp.einsum(
        "hqk,qhe->khe",
        attn_probs.astype(jnp.bfloat16),
        grad_attended,
        preferred_element_type=jnp.float32,
    )
    grad_probs = jnp.einsum(
        "qhe,khe->hqk", grad_attended, value_rows, preferred_element_type=jnp.float32
    )
    inner_sum = jnp.sum(attn_probs * grad_probs, axis=-1, keepdims=True)
    grad_scores = (attn_probs * (grad_probs - inner_sum)).astype(jnp.bfloat16)
    grad_queries = (
        jnp.einsum("hqk,khe->qhe", grad_scores, key_rows, preferred_element_type=jnp.float32)
        * score_scale
    )
    grad_keys = (
        jnp.einsum("hqk,qhe->khe", grad_scores, queries, preferred_element_type=jnp.float32)
        * score_scale
    )
    grad_bias = jnp.einsum(
        "bn,hn->bh",
        bucket_hot,
        grad_scores.reshape(head_count, row_count * row_count),
        preferred_element_type=jnp.float32,
    )
    grad_qkv = jnp.concatenate(
        [
            grad_queries.reshape(row_count, model_width),
            grad_keys.reshape(row_count, model_width),
            grad_values.reshape(row_count, model_width),
        ],
        axis=1,
    ).astype(jnp.bfloat16)
    grad_attn_qkv = jnp.einsum(
        "td,tf->df", normed_low, grad_qkv, preferred_element_type=jnp.float32
    )
    grad_normed = jnp.dot(grad_qkv, full_qkv.T, preferred_element_type=jnp.float32)
    grad_inputs_norm, grad_gain_attn = attn_norm_pull(grad_normed)
    grad_in = grad_middle + grad_inputs_norm
    stacked = jnp.concatenate(
        [
            grad_attn_qkv.astype(jnp.bfloat16),
            grad_attn_out.astype(jnp.bfloat16),
            grad_router.astype(jnp.bfloat16),
            jnp.zeros((model_width, full_width - dense_width), jnp.bfloat16),
        ],
        axis=1,
    )
    if direct:
        small = jnp.concatenate([grad_gain_attn, grad_gain_ffn, grad_bias.reshape(-1)])
        small_size = small.shape[0]
        small_rows = -(-small_size // (8 * lane_count)) * 8
        small = jnp.pad(small, (0, small_rows * lane_count - small_size))
        owned, small = reduce_rows(
            stacked.reshape(-1, shard_rows, full_width), small.reshape(small_rows, lane_count)
        )
        small = small.reshape(-1)
        grad_gain_attn = small[:model_width]
        grad_gain_ffn = small[model_width : 2 * model_width]
        grad_bias = small[2 * model_width : small_size].reshape(bucket_count, head_count)
    else:
        pieces = lax.all_to_all(
            stacked.reshape(group_count, dp_count * shard_rows, full_width),
            "exp",
            split_axis=0,
            concat_axis=0,
            tiled=True,
        ).astype(jnp.float32)
        pieces = jnp.sum(pieces, axis=0).reshape(dp_count, shard_rows, full_width)
        pieces = lax.all_to_all(
            pieces.astype(jnp.bfloat16), "dp", split_axis=0, concat_axis=0, tiled=True
        ).astype(jnp.float32)
        owned = jnp.sum(pieces, axis=0)
        grad_gain_attn, grad_gain_ffn, grad_bias = lax.psum(
            (grad_gain_attn, grad_gain_ffn, grad_bias), ("exp", "dp")
        )
    grad_attn_qkv = owned[:, : 3 * model_width]
    grad_attn_out = owned[:, 3 * model_width : 4 * model_width]
    grad_router = owned[:, 4 * model_width : dense_width]
    return (
        mixed,
        grad_in,
        grad_gain_attn,
        grad_attn_qkv,
        grad_attn_out,
        grad_bias,
        grad_gain_ffn,
        grad_router,
        grad_expert_in,
        grad_expert_out,
    )


def solution(mesh):
    return jax.shard_map(
        local,
        mesh=mesh,
        in_specs=(
            P(("exp", "dp"), None),
            P(("exp", "dp"), None),
            P(("exp", "dp"), None),
            P(("exp", "dp"), None),
            P(),
            P(("exp", "dp"), None),
            P(("exp", "dp"), None),
            P(),
            P(),
            P(("exp", "dp"), None),
            P("exp", None, "dp"),
            P("exp", "dp", None),
        ),
        out_specs=(
            P(("exp", "dp"), None),
            P(("exp", "dp"), None),
            P(),
            P(("exp", "dp"), None),
            P(("exp", "dp"), None),
            P(),
            P(),
            P(("exp", "dp"), None),
            P("exp", None, "dp"),
            P("exp", "dp", None),
        ),
        check_vma=False,
    )
```

```python
import functools

import jax
import jax.numpy as jnp
import numpy as np
from jax import lax
from jax.experimental import pallas as pl
from jax.experimental.pallas import tpu as pltpu
from jax.sharding import PartitionSpec as P

MESH = pl.DeviceIdType.MESH
lane_count = 128
by_y = (0, 3)

epsilon = 1e-06


def bucket_table(row_count, bucket_count):
    offset = np.arange(row_count)[None, :] - np.arange(row_count)[:, None]
    half_count = bucket_count // 2
    exact_count = half_count // 2
    spread = np.abs(offset)
    scaled = (
        np.log(np.maximum(spread, 1) / exact_count)
        / np.log(128.0 / exact_count)
        * (half_count - exact_count)
    )
    distant = np.minimum(exact_count + np.maximum(scaled, 0.0).astype(np.int32), half_count - 1)
    return ((offset > 0) * half_count + np.where(spread < exact_count, spread, distant)).astype(
        np.int32
    )


def rms_norm(values, gain_vec):
    return (
        values * lax.rsqrt(jnp.mean(values * values, axis=-1, keepdims=True) + epsilon) * gain_vec
    )


def gelu_tanh(values):
    return jax.nn.gelu(values, approximate=True)


def segment_ids(lengths, row_count):
    boundary = jnp.cumsum(lengths, axis=-1)
    position = jnp.arange(row_count, dtype=jnp.int32)
    return jnp.sum((position[:, None] >= boundary[..., None, :]).astype(jnp.int32), axis=-1)


def score_block(queries, key_rows, pos_bias, allowed, score_scale):
    scores = (
        jnp.einsum("qhe,khe->hqk", queries, key_rows, preferred_element_type=jnp.float32)
        * score_scale
        + pos_bias
    )
    return jnp.where(allowed, scores, -1e30)


def positions():
    e, z = lax.axis_index("exp"), lax.axis_index("dp")
    core, side_x, side_y = lax.rem(e, 2), lax.rem(lax.div(e, 2), 2), lax.div(e, 4)
    step_core, step_x, step_y = 1 - 2 * core, 2 - 4 * side_x, 4 - 8 * side_y
    chips = (e, e + step_x, e + step_y, e + step_x + step_y)
    return e, z, step_core, chips


def greet(devices):
    barrier = pltpu.get_barrier_semaphore()
    for device in devices:
        pl.semaphore_signal(barrier, inc=1, device_id=device, device_id_type=MESH)
    pl.semaphore_wait(barrier, len(devices))


def gather_kernel(mine_ref, full_ref, local_sem, send_sem, recv_sem):
    e, z, step_core, chips = positions()
    zs = [lax.rem(z + j, 4) for j in range(4)]
    partner = (e + step_core, z)
    beside = {1: (chips[1], z), 2: (chips[2], z)}
    along = {j: (e, zs[j]) for j in (1, 2, 3)}
    greet([partner, beside[1], beside[2], along[1], along[2], along[3]])
    sends = []

    def send(src, chip, j, device, recv):
        copy = pltpu.make_async_remote_copy(
            src_ref=src,
            dst_ref=full_ref.at[chips[chip] * 4 + zs[j]],
            send_sem=send_sem.at[len(sends)],
            recv_sem=recv_sem.at[recv],
            device_id=device,
            device_id_type=MESH,
        )
        copy.start()
        sends.append(copy)

    def held(chip, j):
        return full_ref.at[chips[chip] * 4 + zs[j]]

    def arrive(place, recv):
        pltpu.make_async_remote_copy(
            src_ref=place,
            dst_ref=place,
            send_sem=send_sem.at[0],
            recv_sem=recv_sem.at[recv],
            device_id=partner,
            device_id_type=MESH,
        ).wait_recv()

    def spread(src, j):
        send(src, 0, j, beside[1], 4 + j)
        send(src, 0, j, beside[2], 8 + j)
        send(src, 0, j, partner, 16 + j)

    def from_x(j):
        arrive(held(1, j), 4 + j)
        if j in by_y:
            send(held(1, j), 1, j, beside[2], 12 + j)
        send(held(1, j), 1, j, partner, 20 + j)

    def from_y(j):
        arrive(held(2, j), 8 + j)
        if j not in by_y:
            send(held(2, j), 2, j, beside[1], 12 + j)
        send(held(2, j), 2, j, partner, 24 + j)

    own = pltpu.make_async_copy(mine_ref, held(0, 0), local_sem)
    own.start()
    for j in (1, 3, 2):
        send(mine_ref, 0, 0, along[j], (4 - j) % 4)
    spread(mine_ref, 0)
    for j in (3, 1):
        arrive(held(0, j), j)
        spread(held(0, j), j)
    from_x(0)
    from_y(0)
    arrive(held(0, 2), 2)
    spread(held(0, 2), 2)
    for j in (3, 1, 2):
        from_x(j)
        from_y(j)
    for j in (0, 3, 1, 2):
        arrive(held(3, j), 12 + j)
        send(held(3, j), 3, j, partner, 28 + j)
    for chip in range(4):
        for j in range(4):
            arrive(full_ref.at[(chips[chip] + step_core) * 4 + zs[j]], 16 + chip * 4 + j)
    for copy in sends:
        copy.wait_send()
    own.wait()


def gather_rows(mine):
    rows, width = mine.shape
    full = pl.pallas_call(
        gather_kernel,
        out_shape=jax.ShapeDtypeStruct((32, rows, width), mine.dtype),
        in_specs=[pl.BlockSpec(memory_space=pl.ANY)],
        out_specs=pl.BlockSpec(memory_space=pl.ANY),
        scratch_shapes=[
            pltpu.SemaphoreType.DMA,
            pltpu.SemaphoreType.DMA((31,)),
            pltpu.SemaphoreType.DMA((32,)),
        ],
        compiler_params=pltpu.CompilerParams(collective_id=0, has_side_effects=True),
        cost_estimate=pl.CostEstimate(flops=0, bytes_accessed=64 * rows * width, transcendentals=0),
        name="gather_rows",
    )(mine)
    return full.reshape(32 * rows, width)


def reduce_kernel(
    normed_ref, attended_ref, ffn_ref, qkv_ref, branch_ref, logit_ref, small_ref,
    out_ref, total_ref,
    grad_ref, from_core, summed, passing, from_x, from_y, from_z,
    small_sum, small_in, small_z, send_sem, recv_sem, small_send, small_recv,
):
    e, z, step_core, chips = positions()
    zs = [lax.rem(z + j, 4) for j in range(4)]
    partner = (e + step_core, z)
    beside = {1: (chips[1], z), 2: (chips[2], z)}
    along = {j: (e, zs[j]) for j in (1, 2, 3)}
    greet([partner, beside[1], beside[2], along[1], along[2], along[3]])
    sends = []

    def send(src, dst, device, recv):
        copy = pltpu.make_async_remote_copy(
            src_ref=src,
            dst_ref=dst,
            send_sem=send_sem.at[len(sends)],
            recv_sem=recv_sem.at[recv],
            device_id=device,
            device_id_type=MESH,
        )
        copy.start()
        sends.append(copy)

    def small_copy(src, dst, device, number, recv):
        return pltpu.make_async_remote_copy(
            src_ref=src,
            dst_ref=dst,
            send_sem=small_send.at[number],
            recv_sem=small_recv.at[recv],
            device_id=device,
            device_id_type=MESH,
        )

    def arrive(place, recv):
        pltpu.make_async_remote_copy(
            src_ref=place,
            dst_ref=place,
            send_sem=send_sem.at[0],
            recv_sem=recv_sem.at[recv],
            device_id=partner,
            device_id_type=MESH,
        ).wait_recv()
        return place[...].astype(jnp.float32)

    def pair(chip, j):
        number = chip * 4 + j
        mine = grad_ref[chips[chip] * 4 + zs[j]].astype(jnp.float32)
        return mine + arrive(from_core.at[number], number)

    def step_sum(number, device):
        copy = small_copy(small_sum.at[number], small_in.at[number], device, number, number)
        copy.start()
        copy.wait_recv()
        small_sum[number + 1] = small_sum[number] + small_in[number]
        return copy

    def make(chip):
        count = normed_ref.shape[0] // 4
        group = lax.div(chips[chip], 2)
        here = pl.ds(pl.multiple_of(group * count, count), count)
        column = 0
        for left, right in ((normed_ref, qkv_ref), (attended_ref, branch_ref), (ffn_ref, logit_ref)):
            width = right.shape[1]
            step = width if width <= 768 else 768
            for start in range(0, width, step):
                part = jnp.dot(
                    left[here, :], right[:, start : start + step],
                    preferred_element_type=jnp.float32,
                )
                part = part.reshape(8, count // 8, step).astype(jnp.bfloat16)
                grad_ref[pl.ds(group * 8, 8), :, column + start : column + start + step] = part
            column += width

    def diagonal(j):
        number = 12 + j
        summed[number] = pair(3, j).astype(jnp.bfloat16)
        device = beside[2] if j in by_y else beside[1]
        send(summed.at[number], passing.at[j], device, 16 + j)

    def beside_chips(j):
        for chip in (2, 1) if j in by_y else (1, 2):
            number = chip * 4 + j
            value = pair(chip, j)
            if (j in by_y) == (chip == 1):
                value = value + arrive(passing.at[j], 16 + j)
            summed[number] = value.astype(jnp.bfloat16)
            landing = from_x if chip == 1 else from_y
            send(summed.at[number], landing.at[j], beside[chip], 16 + number)

    def own_chip(j):
        value = pair(0, j) + arrive(from_x.at[j], 20 + j) + arrive(from_y.at[j], 24 + j)
        if j == 0:
            for other in (1, 2, 3):
                value = value + arrive(from_z.at[other - 1], 27 + other)
            out_ref[...] = value
        else:
            summed[j] = value.astype(jnp.bfloat16)
            send(summed.at[j], from_z.at[3 - j], along[j], 31 - j)

    order = (2, 1, 3, 0)
    small_sum[0] = small_ref[...]
    for chip in (3, 1, 2, 0):
        make(chip)
        for j in order[:2]:
            place = (chips[chip] + step_core) * 4 + zs[j]
            send(grad_ref.at[place], from_core.at[chip * 4 + j], partner, chip * 4 + j)
    for j in order[2:]:
        for chip in (3, 1, 2, 0):
            place = (chips[chip] + step_core) * 4 + zs[j]
            send(grad_ref.at[place], from_core.at[chip * 4 + j], partner, chip * 4 + j)
    diagonal(order[0])
    diagonal(order[1])
    beside_chips(order[0])
    small_copies = [step_sum(0, partner)]
    diagonal(order[2])
    beside_chips(order[1])
    own_chip(order[0])
    small_copies.append(step_sum(1, beside[1]))
    diagonal(order[3])
    beside_chips(order[2])
    own_chip(order[1])
    small_copies.append(step_sum(2, beside[2]))
    beside_chips(order[3])
    small_z[0] = small_sum[3]
    for j in (1, 2, 3):
        copy = small_copy(small_z.at[0], small_z.at[4 - j], along[j], 2 + j, 6 - j)
        copy.start()
        small_copies.append(copy)
    own_chip(order[2])
    own_chip(order[3])
    for copy in small_copies[3:]:
        copy.wait_recv()
    spot = [lax.rem(4 + k - z, 4) for k in range(4)]
    total_ref[...] = (small_z[spot[0]] + small_z[spot[1]]) + (small_z[spot[2]] + small_z[spot[3]])
    for copy in sends + small_copies:
        copy.wait_send()


def reduce_rows(operands, rows, small):
    width = sum(right.shape[1] for right in operands[3:])
    vmem = pl.BlockSpec(memory_space=pltpu.VMEM)
    block = functools.partial(pltpu.VMEM, dtype=jnp.bfloat16)
    return pl.pallas_call(
        reduce_kernel,
        out_shape=(
            jax.ShapeDtypeStruct((rows, width), jnp.float32),
            jax.ShapeDtypeStruct(small.shape, jnp.float32),
        ),
        in_specs=[vmem] * 7,
        out_specs=(vmem, vmem),
        scratch_shapes=[
            block((32, rows, width)),
            block((16, rows, width)),
            block((16, rows, width)),
            block((4, rows, width)),
            block((4, rows, width)),
            block((4, rows, width)),
            block((3, rows, width)),
            pltpu.VMEM((4,) + small.shape, jnp.float32),
            pltpu.VMEM((3,) + small.shape, jnp.float32),
            pltpu.VMEM((4,) + small.shape, jnp.float32),
            pltpu.SemaphoreType.DMA((31,)),
            pltpu.SemaphoreType.DMA((31,)),
            pltpu.SemaphoreType.DMA((6,)),
            pltpu.SemaphoreType.DMA((6,)),
        ],
        compiler_params=pltpu.CompilerParams(
            collective_id=1, has_side_effects=True, vmem_limit_bytes=40 * 1024 * 1024
        ),
        cost_estimate=pl.CostEstimate(
            flops=8192 * rows * width, bytes_accessed=4 * rows * width, transcendentals=0
        ),
        name="reduce_rows",
    )(*operands, small)


def line_copy(src, dst, sems, number, device):
    return pltpu.make_async_remote_copy(
        src_ref=src,
        dst_ref=dst,
        send_sem=sems[0].at[number],
        recv_sem=sems[1].at[number],
        device_id=device,
        device_id_type=MESH,
    )


def plane_places():
    e, z, step_core, chips = positions()
    places = [(a, h, chips[a] + h * step_core) for a in range(4) for h in range(2)]
    return e, z, chips, places[1:]


def dispatch_kernel(
    out_ref, full_ref, plane_send, plane_recv, up_send, up_recv, down_send, down_recv
):
    e, z, chips, places = plane_places()
    greet([(d, z) for _, _, d in places] + [(e, lax.rem(z + t, 4)) for t in (1, 2, 3)])
    lines = (((up_send, up_recv), 1), ((down_send, down_recv), -1))
    pairs = [lax.div(chip, 2) * 2 for chip in chips]
    plane = []
    for a, h, device in places:
        copy = line_copy(
            out_ref.at[device], full_ref.at[z * 8 + e], (plane_send, plane_recv), a * 2 + h,
            (device, z),
        )
        copy.start()
        plane.append(copy)
    full_ref[z * 8 + e] = out_ref[e]

    def inside(depth):
        return (depth >= 0) & (depth <= 3)

    def hop(line, sign, step, a):
        block = full_ref.at[pl.ds((z - sign * step) * 8 + pairs[a], 2)]
        return line_copy(block, block, line, step * 4 + a, (e, z + sign))

    def landed(line, sign, step, a):
        block = full_ref.at[pl.ds((z - sign * (step + 1)) * 8 + pairs[a], 2)]
        return line_copy(block, block, line, step * 4 + a, (e, z - sign))

    for step in range(4):
        for a in range(4):
            if step == 0:
                for copy, (chip, _, _) in zip(plane, places):
                    if chip == a:
                        copy.wait_recv()
            for line, sign in lines:
                if step > 0:

                    @pl.when(inside(z - sign * step))
                    def _(line=line, sign=sign, step=step, a=a):
                        landed(line, sign, step - 1, a).wait_recv()

                if step < 3:

                    @pl.when(inside(z - sign * step) & inside(z + sign))
                    def _(line=line, sign=sign, step=step, a=a):
                        hop(line, sign, step, a).start()

    for copy in plane:
        copy.wait_send()
    for step in range(3):
        for line, sign in lines:

            @pl.when(inside(z - sign * step) & inside(z + sign))
            def _(line=line, sign=sign, step=step):
                for a in range(4):
                    hop(line, sign, step, a).wait_send()


def return_kernel(
    part_ref, back_ref, leaving, arriving, result,
    plane_send, plane_recv, up_send, up_recv, down_send, down_recv,
):
    e, z, chips, places = plane_places()
    greet([(d, z) for _, _, d in places] + [(e, lax.rem(z + t, 4)) for t in (1, 2, 3)])
    lines = (((up_send, up_recv), 1), ((down_send, down_recv), -1))
    pairs = [lax.div(chip, 2) * 2 for chip in chips]

    def inside(depth):
        return (depth >= 0) & (depth <= 3)

    def hop(way, ahead, a):
        line, sign = lines[way]
        return line_copy(
            leaving.at[way, ahead - 1, a], arriving.at[way, ahead - 1, a], line,
            (ahead - 1) * 4 + a, (e, z + sign),
        )

    def landed(way, ahead, a):
        line, sign = lines[way]
        place = arriving.at[way, ahead, a]
        line_copy(place, place, line, ahead * 4 + a, (e, z - sign)).wait_recv()
        return place[...].astype(jnp.float32)

    def own(depth, a):
        return part_ref[pl.ds(depth * 8 + pairs[a], 2)]

    for ahead in (3, 2, 1):
        for a in (3, 1, 2, 0):
            for way, (_, sign) in enumerate(lines):

                @pl.when(inside(z + sign * ahead))
                def _(way=way, sign=sign, ahead=ahead, a=a):
                    leaving[way, ahead - 1, a] = own(z + sign * ahead, a)
                    if ahead < 3:

                        @pl.when(inside(z - sign))
                        def _():
                            value = own(z + sign * ahead, a).astype(jnp.float32)
                            value = value + landed(way, ahead, a)
                            leaving[way, ahead - 1, a] = value.astype(jnp.bfloat16)

                    hop(way, ahead, a).start()

    plane = []
    for a in (3, 1, 2, 0):
        result[a] = own(z, a).astype(jnp.float32)
        for way, (_, sign) in enumerate(lines):

            @pl.when(inside(z - sign))
            def _(way=way, a=a):
                result[a] = result[a] + landed(way, 0, a)

        for core in range(2):
            leaving[0, 3, a, core] = result[a, core].astype(jnp.bfloat16)
        for chip, h, device in places:
            if chip == a:
                copy = line_copy(
                    leaving.at[0, 3, a, lax.rem(device, 2)], back_ref.at[e],
                    (plane_send, plane_recv), a * 2 + h, (device, z),
                )
                copy.start()
                plane.append(copy)
    back_ref[e] = leaving[0, 3, 0, lax.rem(e, 2)]
    for copy in plane:
        copy.wait_recv()
    for copy in plane:
        copy.wait_send()
    for ahead in (3, 2, 1):
        for way, (_, sign) in enumerate(lines):

            @pl.when(inside(z + sign * ahead))
            def _(way=way, ahead=ahead):
                for a in range(4):
                    hop(way, ahead, a).wait_send()


def line_call(kernel, operand, blocks, scratch, number, name):
    _, rows, width = operand.shape
    vmem = pl.BlockSpec(memory_space=pltpu.VMEM)
    return pl.pallas_call(
        kernel,
        out_shape=jax.ShapeDtypeStruct((blocks, rows, width), operand.dtype),
        in_specs=[vmem],
        out_specs=vmem,
        scratch_shapes=scratch
        + [pltpu.SemaphoreType.DMA((8,))] * 2
        + [pltpu.SemaphoreType.DMA((12,))] * 4,
        compiler_params=pltpu.CompilerParams(
            collective_id=number, has_side_effects=True, vmem_limit_bytes=40 * 1024 * 1024
        ),
        cost_estimate=pl.CostEstimate(
            flops=0, bytes_accessed=80 * rows * width, transcendentals=0
        ),
        name=name,
    )(operand)


def dispatch_rows(outgoing):
    return line_call(dispatch_kernel, outgoing, 32, [], 2, "dispatch_rows")


def return_rows(partial):
    _, rows, width = partial.shape
    scratch = [
        pltpu.VMEM((2, 4, 4, 2, rows, width), partial.dtype),
        pltpu.VMEM((2, 3, 4, 2, rows, width), partial.dtype),
        pltpu.VMEM((4, 2, rows, width), jnp.float32),
    ]
    return line_call(return_kernel, partial, 8, scratch, 3, "return_rows")


def local(
    hidden_in,
    cotangent,
    lengths,
    routes,
    gain_attn,
    attn_qkv,
    attn_out,
    rel_bias,
    gain_ffn,
    router,
    expert_in,
    expert_out,
):
    row_count, model_width = hidden_in.shape
    bucket_count, head_count = rel_bias.shape
    head_size = model_width // head_count
    score_scale = head_size ** (-0.5)
    expert_count = router.shape[1]
    group_count = lax.axis_size("exp")
    local_count = expert_in.shape[0]
    capacity = max(2, row_count * 5 // (4 * expert_count))
    dp_count = lax.axis_size("dp")
    shard_rows = attn_qkv.shape[0]
    direct = group_count == 8 and dp_count == 4 and shard_rows % 8 == 0
    dense_width = 4 * model_width + expert_count
    full_width = -(-dense_width // lane_count) * lane_count
    shard = jnp.concatenate(
        [
            attn_qkv,
            attn_out,
            router,
            jnp.zeros((shard_rows, full_width - dense_width), jnp.bfloat16),
        ],
        axis=1,
    )
    if direct:
        full = gather_rows(shard)
    else:
        full = lax.all_gather(shard, ("exp", "dp"), axis=0, tiled=True)
    full_qkv = full[:, : 3 * model_width]
    full_out = full[:, 3 * model_width : 4 * model_width]
    full_route = full[:, 4 * model_width : dense_width]
    inputs = hidden_in.astype(jnp.float32)
    normed, attn_norm_pull = jax.vjp(rms_norm, inputs, gain_attn)
    normed_low = normed.astype(jnp.bfloat16)
    qkv_low = jnp.dot(normed_low, full_qkv, preferred_element_type=jnp.float32).astype(jnp.bfloat16)
    queries = qkv_low[:, :model_width].reshape(row_count, head_count, head_size)
    key_rows = qkv_low[:, model_width : 2 * model_width].reshape(row_count, head_count, head_size)
    value_rows = qkv_low[:, 2 * model_width :].reshape(row_count, head_count, head_size)
    bucket_ids = bucket_table(row_count, bucket_count)
    bucket_hot = jnp.asarray(
        bucket_ids.reshape(1, -1) == np.arange(bucket_count)[:, None], dtype=jnp.bfloat16
    )
    pos_bias = jnp.einsum(
        "bh,bn->hn",
        rel_bias,
        bucket_hot.astype(jnp.float32),
        precision=lax.Precision.HIGHEST,
    ).reshape(head_count, row_count, row_count)
    segment = segment_ids(lengths, row_count)[0]
    allowed = (segment[:, None] == segment[None, :])[None]
    scores = score_block(queries, key_rows, pos_bias, allowed, score_scale)
    row_max = jnp.max(scores, axis=-1, keepdims=True)
    log_total = row_max + jnp.log(jnp.sum(jnp.exp(scores - row_max), axis=-1, keepdims=True))
    attn_probs = jnp.exp(scores - log_total)
    attended = jnp.einsum(
        "hqk,khe->qhe",
        attn_probs.astype(jnp.bfloat16),
        value_rows,
        preferred_element_type=jnp.float32,
    )
    attended_low = attended.reshape(row_count, model_width).astype(jnp.bfloat16)
    middle = inputs + jnp.dot(attended_low, full_out, preferred_element_type=jnp.float32)
    ffn_norm, ffn_norm_pull = jax.vjp(rms_norm, middle, gain_ffn)
    ffn_low = ffn_norm.astype(jnp.bfloat16)
    gate_probs = jax.nn.softmax(
        jnp.dot(ffn_low, full_route, preferred_element_type=jnp.float32), axis=-1
    )
    choose = routes == jnp.arange(expert_count, dtype=jnp.int32)[None, :]
    gate_prob = jnp.sum(jnp.where(choose, gate_probs, 0.0), axis=1, keepdims=True)
    earlier = jnp.asarray(np.tril(np.ones((row_count, row_count)), -1), dtype=jnp.bfloat16)
    rank_index = jnp.dot(earlier, choose.astype(jnp.bfloat16), preferred_element_type=jnp.float32)
    slot_index = jnp.sum(jnp.where(choose, rank_index, 0.0), axis=1).astype(jnp.int32)
    half_rows = local_count * capacity
    group_place = routes[:, 0] // local_count * half_rows
    slot_place = routes[:, 0] * capacity + slot_index + group_place
    dispatch = (
        jnp.arange(2 * group_count * half_rows, dtype=jnp.int32)[:, None]
        == jnp.concatenate([slot_place, slot_place + half_rows])[None, :]
    ).astype(jnp.bfloat16)
    grad_out = cotangent.astype(jnp.float32)
    grad_picked = (gate_prob * grad_out).astype(jnp.bfloat16)
    outgoing = jnp.dot(
        dispatch,
        jnp.concatenate([ffn_low, grad_picked], axis=0),
        preferred_element_type=jnp.float32,
    ).astype(jnp.bfloat16)
    outgoing = outgoing.reshape(group_count, 2 * half_rows, model_width)
    if direct:
        gathered = dispatch_rows(outgoing)
    else:
        arrived = lax.all_to_all(outgoing, "exp", split_axis=0, concat_axis=0, tiled=True)
        gathered = lax.all_gather(arrived, "dp", axis=0, tiled=True)
    slot_rows = dp_count * group_count * capacity
    gathered = gathered.reshape(-1, 2, local_count, capacity, model_width)
    gathered = jnp.transpose(gathered, (1, 2, 0, 3, 4)).reshape(
        2, local_count, slot_rows, model_width
    )
    expert_rows = gathered[0]
    grad_result = gathered[1]
    hidden_pre = jnp.einsum(
        "lsd,ldf->lsf", expert_rows, expert_in, preferred_element_type=jnp.float32
    )
    active_f32, gelu_pull = jax.vjp(gelu_tanh, hidden_pre)
    active = active_f32.astype(jnp.bfloat16)
    partial_out = jnp.einsum("lsf,lfd->lsd", active, expert_out, preferred_element_type=jnp.float32)
    grad_active = jnp.einsum(
        "lsd,lfd->lsf", grad_result, expert_out, preferred_element_type=jnp.float32
    )
    grad_pre = gelu_pull(grad_active)[0].astype(jnp.bfloat16)
    grad_part = jnp.einsum("lsf,ldf->lsd", grad_pre, expert_in, preferred_element_type=jnp.float32)
    grad_expert_out = jnp.einsum(
        "lsf,lsd->lfd", active, grad_result, preferred_element_type=jnp.float32
    )
    grad_expert_in = jnp.einsum(
        "lsd,lsf->ldf", expert_rows, grad_pre, preferred_element_type=jnp.float32
    )
    partial = jnp.stack(
        [partial_out.astype(jnp.bfloat16), grad_part.astype(jnp.bfloat16)]
    ).reshape(2, local_count, dp_count * group_count, capacity, model_width)
    partial = jnp.transpose(partial, (2, 0, 1, 3, 4)).reshape(-1, 2 * half_rows, model_width)
    if direct:
        returned = return_rows(partial)
    else:
        result_rows = lax.psum_scatter(partial, "dp", scatter_dimension=0, tiled=True)
        returned = lax.all_to_all(result_rows, "exp", split_axis=0, concat_axis=0, tiled=True)
    picked_both = lax.dot_general(
        dispatch,
        returned.reshape(-1, model_width),
        (((0,), (0,)), ((), ())),
        preferred_element_type=jnp.float32,
    )
    picked = picked_both[:row_count]
    grad_ffn = picked_both[row_count:]
    mixed = (middle + gate_prob * picked).astype(jnp.bfloat16)
    gate_grad = jnp.sum(grad_out * picked, axis=1, keepdims=True)
    logit_grad = (gate_probs * (jnp.where(choose, gate_grad, 0.0) - gate_prob * gate_grad)).astype(
        jnp.bfloat16
    )
    grad_ffn = grad_ffn + jnp.dot(logit_grad, full_route.T, preferred_element_type=jnp.float32)
    grad_middle_norm, grad_gain_ffn = ffn_norm_pull(grad_ffn)
    grad_middle = grad_out + grad_middle_norm
    branch_grad = grad_middle.astype(jnp.bfloat16)
    grad_attended = jnp.dot(branch_grad, full_out.T, preferred_element_type=jnp.float32).astype(
        jnp.bfloat16
    )
    grad_attended = grad_attended.reshape(row_count, head_count, head_size)
    scores = score_block(queries, key_rows, pos_bias, allowed, score_scale)
    attn_probs = jnp.exp(scores - log_total)
    grad_values = jnp.einsum(
        "hqk,qhe->khe",
        attn_probs.astype(jnp.bfloat16),
        grad_attended,
        preferred_element_type=jnp.float32,
    )
    grad_probs = jnp.einsum(
        "qhe,khe->hqk", grad_attended, value_rows, preferred_element_type=jnp.float32
    )
    inner_sum = jnp.sum(attn_probs * grad_probs, axis=-1, keepdims=True)
    grad_scores = (attn_probs * (grad_probs - inner_sum)).astype(jnp.bfloat16)
    grad_queries = (
        jnp.einsum("hqk,khe->qhe", grad_scores, key_rows, preferred_element_type=jnp.float32)
        * score_scale
    )
    grad_keys = (
        jnp.einsum("hqk,qhe->khe", grad_scores, queries, preferred_element_type=jnp.float32)
        * score_scale
    )
    grad_bias = jnp.einsum(
        "bn,hn->bh",
        bucket_hot,
        grad_scores.reshape(head_count, row_count * row_count),
        preferred_element_type=jnp.float32,
    )
    grad_qkv = jnp.concatenate(
        [
            grad_queries.reshape(row_count, model_width),
            grad_keys.reshape(row_count, model_width),
            grad_values.reshape(row_count, model_width),
        ],
        axis=1,
    ).astype(jnp.bfloat16)
    grad_normed = jnp.dot(grad_qkv, full_qkv.T, preferred_element_type=jnp.float32)
    grad_inputs_norm, grad_gain_attn = attn_norm_pull(grad_normed)
    grad_in = grad_middle + grad_inputs_norm
    padded_logit = jnp.pad(logit_grad, ((0, 0), (0, full_width - dense_width)))
    dense_pairs = ((normed_low, grad_qkv), (attended_low, branch_grad), (ffn_low, padded_logit))
    if direct:
        small = jnp.concatenate([grad_gain_attn, grad_gain_ffn, grad_bias.reshape(-1)])
        small_size = small.shape[0]
        small_rows = -(-small_size // (8 * lane_count)) * 8
        small = jnp.pad(small, (0, small_rows * lane_count - small_size))
        owned, small = reduce_rows(
            [left.T for left, _ in dense_pairs] + [right for _, right in dense_pairs],
            shard_rows,
            small.reshape(small_rows, lane_count),
        )
        small = small.reshape(-1)
        grad_gain_attn = small[:model_width]
        grad_gain_ffn = small[model_width : 2 * model_width]
        grad_bias = small[2 * model_width : small_size].reshape(bucket_count, head_count)
    else:
        stacked = jnp.concatenate(
            [
                jnp.einsum("td,te->de", left, right, preferred_element_type=jnp.float32).astype(
                    jnp.bfloat16
                )
                for left, right in dense_pairs
            ],
            axis=1,
        )
        pieces = lax.all_to_all(
            stacked.reshape(group_count, dp_count * shard_rows, full_width),
            "exp",
            split_axis=0,
            concat_axis=0,
            tiled=True,
        ).astype(jnp.float32)
        pieces = jnp.sum(pieces, axis=0).reshape(dp_count, shard_rows, full_width)
        pieces = lax.all_to_all(
            pieces.astype(jnp.bfloat16), "dp", split_axis=0, concat_axis=0, tiled=True
        ).astype(jnp.float32)
        owned = jnp.sum(pieces, axis=0)
        grad_gain_attn, grad_gain_ffn, grad_bias = lax.psum(
            (grad_gain_attn, grad_gain_ffn, grad_bias), ("exp", "dp")
        )
    grad_attn_qkv = owned[:, : 3 * model_width]
    grad_attn_out = owned[:, 3 * model_width : 4 * model_width]
    grad_router = owned[:, 4 * model_width : dense_width]
    return (
        mixed,
        grad_in,
        grad_gain_attn,
        grad_attn_qkv,
        grad_attn_out,
        grad_bias,
        grad_gain_ffn,
        grad_router,
        grad_expert_in,
        grad_expert_out,
    )


def solution(mesh):
    return jax.shard_map(
        local,
        mesh=mesh,
        in_specs=(
            P(("exp", "dp"), None),
            P(("exp", "dp"), None),
            P(("exp", "dp"), None),
            P(("exp", "dp"), None),
            P(),
            P(("exp", "dp"), None),
            P(("exp", "dp"), None),
            P(),
            P(),
            P(("exp", "dp"), None),
            P("exp", None, "dp"),
            P("exp", "dp", None),
        ),
        out_specs=(
            P(("exp", "dp"), None),
            P(("exp", "dp"), None),
            P(),
            P(("exp", "dp"), None),
            P(("exp", "dp"), None),
            P(),
            P(),
            P(("exp", "dp"), None),
            P("exp", None, "dp"),
            P("exp", "dp", None),
        ),
        check_vma=False,
    )
```

```python
import functools

import jax
import jax.numpy as jnp
import numpy as np
from jax import lax
from jax.experimental import pallas as pl
from jax.experimental.pallas import tpu as pltpu
from jax.sharding import PartitionSpec as P

MESH = pl.DeviceIdType.MESH
lane_count = 128
by_y = (0, 3)

epsilon = 1e-06


def bucket_table(row_count, bucket_count):
    offset = np.arange(row_count)[None, :] - np.arange(row_count)[:, None]
    half_count = bucket_count // 2
    exact_count = half_count // 2
    spread = np.abs(offset)
    scaled = (
        np.log(np.maximum(spread, 1) / exact_count)
        / np.log(128.0 / exact_count)
        * (half_count - exact_count)
    )
    distant = np.minimum(exact_count + np.maximum(scaled, 0.0).astype(np.int32), half_count - 1)
    return ((offset > 0) * half_count + np.where(spread < exact_count, spread, distant)).astype(
        np.int32
    )


def rms_norm(values, gain_vec):
    return (
        values * lax.rsqrt(jnp.mean(values * values, axis=-1, keepdims=True) + epsilon) * gain_vec
    )


def gelu_tanh(values):
    return jax.nn.gelu(values, approximate=True)


def segment_ids(lengths, row_count):
    boundary = jnp.cumsum(lengths, axis=-1)
    position = jnp.arange(row_count, dtype=jnp.int32)
    return jnp.sum((position[:, None] >= boundary[..., None, :]).astype(jnp.int32), axis=-1)


def positions():
    e, z = lax.axis_index("exp"), lax.axis_index("dp")
    core, side_x, side_y = lax.rem(e, 2), lax.rem(lax.div(e, 2), 2), lax.div(e, 4)
    step_core, step_x, step_y = 1 - 2 * core, 2 - 4 * side_x, 4 - 8 * side_y
    chips = (e, e + step_x, e + step_y, e + step_x + step_y)
    return e, z, step_core, chips


def greet(devices):
    barrier = pltpu.get_barrier_semaphore()
    for device in devices:
        pl.semaphore_signal(barrier, inc=1, device_id=device, device_id_type=MESH)
    pl.semaphore_wait(barrier, len(devices))


def gather_kernel(mine_ref, full_ref, local_sem, send_sem, recv_sem):
    e, z, step_core, chips = positions()
    zs = [lax.rem(z + j, 4) for j in range(4)]
    partner = (e + step_core, z)
    beside = {1: (chips[1], z), 2: (chips[2], z)}
    along = {j: (e, zs[j]) for j in (1, 2, 3)}
    greet([partner, beside[1], beside[2], along[1], along[2], along[3]])
    sends = []

    def send(src, chip, j, device, recv):
        copy = pltpu.make_async_remote_copy(
            src_ref=src,
            dst_ref=full_ref.at[chips[chip] * 4 + zs[j]],
            send_sem=send_sem.at[len(sends)],
            recv_sem=recv_sem.at[recv],
            device_id=device,
            device_id_type=MESH,
        )
        copy.start()
        sends.append(copy)

    def held(chip, j):
        return full_ref.at[chips[chip] * 4 + zs[j]]

    def arrive(place, recv):
        pltpu.make_async_remote_copy(
            src_ref=place,
            dst_ref=place,
            send_sem=send_sem.at[0],
            recv_sem=recv_sem.at[recv],
            device_id=partner,
            device_id_type=MESH,
        ).wait_recv()

    def spread(src, j):
        send(src, 0, j, beside[1], 4 + j)
        send(src, 0, j, beside[2], 8 + j)
        send(src, 0, j, partner, 16 + j)

    def from_x(j):
        arrive(held(1, j), 4 + j)
        if j in by_y:
            send(held(1, j), 1, j, beside[2], 12 + j)
        send(held(1, j), 1, j, partner, 20 + j)

    def from_y(j):
        arrive(held(2, j), 8 + j)
        if j not in by_y:
            send(held(2, j), 2, j, beside[1], 12 + j)
        send(held(2, j), 2, j, partner, 24 + j)

    own = pltpu.make_async_copy(mine_ref, held(0, 0), local_sem)
    own.start()
    for j in (1, 3, 2):
        send(mine_ref, 0, 0, along[j], (4 - j) % 4)
    spread(mine_ref, 0)
    for j in (3, 1):
        arrive(held(0, j), j)
        spread(held(0, j), j)
    from_x(0)
    from_y(0)
    arrive(held(0, 2), 2)
    spread(held(0, 2), 2)
    for j in (3, 1, 2):
        from_x(j)
        from_y(j)
    for j in (0, 3, 1, 2):
        arrive(held(3, j), 12 + j)
        send(held(3, j), 3, j, partner, 28 + j)
    for chip in range(4):
        for j in range(4):
            arrive(full_ref.at[(chips[chip] + step_core) * 4 + zs[j]], 16 + chip * 4 + j)
    for copy in sends:
        copy.wait_send()
    own.wait()


def gather_rows(mine):
    rows, width = mine.shape
    full = pl.pallas_call(
        gather_kernel,
        out_shape=jax.ShapeDtypeStruct((32, rows, width), mine.dtype),
        in_specs=[pl.BlockSpec(memory_space=pl.ANY)],
        out_specs=pl.BlockSpec(memory_space=pl.ANY),
        scratch_shapes=[
            pltpu.SemaphoreType.DMA,
            pltpu.SemaphoreType.DMA((31,)),
            pltpu.SemaphoreType.DMA((32,)),
        ],
        compiler_params=pltpu.CompilerParams(collective_id=0, has_side_effects=True),
        cost_estimate=pl.CostEstimate(flops=0, bytes_accessed=64 * rows * width, transcendentals=0),
        name="gather_rows",
    )(mine)
    return full.reshape(32 * rows, width)


def reduce_kernel(
    normed_ref, attended_ref, ffn_ref, qkv_ref, branch_ref, logit_ref, small_ref,
    out_ref, total_ref,
    grad_ref, from_core, summed, passing, from_x, from_y, from_z,
    small_sum, small_in, small_z, send_sem, recv_sem, small_send, small_recv,
):
    e, z, step_core, chips = positions()
    zs = [lax.rem(z + j, 4) for j in range(4)]
    partner = (e + step_core, z)
    beside = {1: (chips[1], z), 2: (chips[2], z)}
    along = {j: (e, zs[j]) for j in (1, 2, 3)}
    greet([partner, beside[1], beside[2], along[1], along[2], along[3]])
    sends = []

    def send(src, dst, device, recv):
        copy = pltpu.make_async_remote_copy(
            src_ref=src,
            dst_ref=dst,
            send_sem=send_sem.at[len(sends)],
            recv_sem=recv_sem.at[recv],
            device_id=device,
            device_id_type=MESH,
        )
        copy.start()
        sends.append(copy)

    def small_copy(src, dst, device, number, recv):
        return pltpu.make_async_remote_copy(
            src_ref=src,
            dst_ref=dst,
            send_sem=small_send.at[number],
            recv_sem=small_recv.at[recv],
            device_id=device,
            device_id_type=MESH,
        )

    def arrive(place, recv):
        pltpu.make_async_remote_copy(
            src_ref=place,
            dst_ref=place,
            send_sem=send_sem.at[0],
            recv_sem=recv_sem.at[recv],
            device_id=partner,
            device_id_type=MESH,
        ).wait_recv()
        return place[...].astype(jnp.float32)

    def pair(chip, j):
        number = chip * 4 + j
        mine = grad_ref[chips[chip] * 4 + zs[j]].astype(jnp.float32)
        return mine + arrive(from_core.at[number], number)

    def step_sum(number, device):
        copy = small_copy(small_sum.at[number], small_in.at[number], device, number, number)
        copy.start()
        copy.wait_recv()
        small_sum[number + 1] = small_sum[number] + small_in[number]
        return copy

    def make(chip):
        count = normed_ref.shape[0] // 4
        group = lax.div(chips[chip], 2)
        here = pl.ds(pl.multiple_of(group * count, count), count)
        column = 0
        for left, right in ((normed_ref, qkv_ref), (attended_ref, branch_ref), (ffn_ref, logit_ref)):
            width = right.shape[1]
            step = width if width <= 768 else 768
            for start in range(0, width, step):
                part = jnp.dot(
                    left[here, :], right[:, start : start + step],
                    preferred_element_type=jnp.float32,
                )
                part = part.reshape(8, count // 8, step).astype(jnp.bfloat16)
                grad_ref[pl.ds(group * 8, 8), :, column + start : column + start + step] = part
            column += width

    def diagonal(j):
        number = 12 + j
        summed[number] = pair(3, j).astype(jnp.bfloat16)
        device = beside[2] if j in by_y else beside[1]
        send(summed.at[number], passing.at[j], device, 16 + j)

    def beside_chips(j):
        for chip in (2, 1) if j in by_y else (1, 2):
            number = chip * 4 + j
            value = pair(chip, j)
            if (j in by_y) == (chip == 1):
                value = value + arrive(passing.at[j], 16 + j)
            summed[number] = value.astype(jnp.bfloat16)
            landing = from_x if chip == 1 else from_y
            send(summed.at[number], landing.at[j], beside[chip], 16 + number)

    def own_chip(j):
        value = pair(0, j) + arrive(from_x.at[j], 20 + j) + arrive(from_y.at[j], 24 + j)
        if j == 0:
            for other in (1, 2, 3):
                value = value + arrive(from_z.at[other - 1], 27 + other)
            out_ref[...] = value
        else:
            summed[j] = value.astype(jnp.bfloat16)
            send(summed.at[j], from_z.at[3 - j], along[j], 31 - j)

    order = (2, 1, 3, 0)
    small_sum[0] = small_ref[...]
    for chip in (3, 1, 2, 0):
        make(chip)
        for j in order[:2]:
            place = (chips[chip] + step_core) * 4 + zs[j]
            send(grad_ref.at[place], from_core.at[chip * 4 + j], partner, chip * 4 + j)
    for j in order[2:]:
        for chip in (3, 1, 2, 0):
            place = (chips[chip] + step_core) * 4 + zs[j]
            send(grad_ref.at[place], from_core.at[chip * 4 + j], partner, chip * 4 + j)
    diagonal(order[0])
    diagonal(order[1])
    beside_chips(order[0])
    small_copies = [step_sum(0, partner)]
    diagonal(order[2])
    beside_chips(order[1])
    own_chip(order[0])
    small_copies.append(step_sum(1, beside[1]))
    diagonal(order[3])
    beside_chips(order[2])
    own_chip(order[1])
    small_copies.append(step_sum(2, beside[2]))
    beside_chips(order[3])
    small_z[0] = small_sum[3]
    for j in (1, 2, 3):
        copy = small_copy(small_z.at[0], small_z.at[4 - j], along[j], 2 + j, 6 - j)
        copy.start()
        small_copies.append(copy)
    own_chip(order[2])
    own_chip(order[3])
    for copy in small_copies[3:]:
        copy.wait_recv()
    spot = [lax.rem(4 + k - z, 4) for k in range(4)]
    total_ref[...] = (small_z[spot[0]] + small_z[spot[1]]) + (small_z[spot[2]] + small_z[spot[3]])
    for copy in sends + small_copies:
        copy.wait_send()


def reduce_rows(operands, rows, small):
    width = sum(right.shape[1] for right in operands[3:])
    vmem = pl.BlockSpec(memory_space=pltpu.VMEM)
    block = functools.partial(pltpu.VMEM, dtype=jnp.bfloat16)
    return pl.pallas_call(
        reduce_kernel,
        out_shape=(
            jax.ShapeDtypeStruct((rows, width), jnp.float32),
            jax.ShapeDtypeStruct(small.shape, jnp.float32),
        ),
        in_specs=[vmem] * 7,
        out_specs=(vmem, vmem),
        scratch_shapes=[
            block((32, rows, width)),
            block((16, rows, width)),
            block((16, rows, width)),
            block((4, rows, width)),
            block((4, rows, width)),
            block((4, rows, width)),
            block((3, rows, width)),
            pltpu.VMEM((4,) + small.shape, jnp.float32),
            pltpu.VMEM((3,) + small.shape, jnp.float32),
            pltpu.VMEM((4,) + small.shape, jnp.float32),
            pltpu.SemaphoreType.DMA((31,)),
            pltpu.SemaphoreType.DMA((31,)),
            pltpu.SemaphoreType.DMA((6,)),
            pltpu.SemaphoreType.DMA((6,)),
        ],
        compiler_params=pltpu.CompilerParams(
            collective_id=1, has_side_effects=True, vmem_limit_bytes=40 * 1024 * 1024
        ),
        cost_estimate=pl.CostEstimate(
            flops=8192 * rows * width, bytes_accessed=4 * rows * width, transcendentals=0
        ),
        name="reduce_rows",
    )(*operands, small)


def line_copy(src, dst, sems, number, device):
    return pltpu.make_async_remote_copy(
        src_ref=src,
        dst_ref=dst,
        send_sem=sems[0].at[number],
        recv_sem=sems[1].at[number],
        device_id=device,
        device_id_type=MESH,
    )


def plane_places():
    e, z, step_core, chips = positions()
    places = [(a, h, chips[a] + h * step_core) for a in range(4) for h in range(2)]
    return e, z, chips, places[1:]


def dispatch_kernel(
    out_ref, full_ref, plane_send, plane_recv, up_send, up_recv, down_send, down_recv
):
    e, z, chips, places = plane_places()
    greet([(d, z) for _, _, d in places] + [(e, lax.rem(z + t, 4)) for t in (1, 2, 3)])
    lines = (((up_send, up_recv), 1), ((down_send, down_recv), -1))
    pairs = [lax.div(chip, 2) * 2 for chip in chips]
    plane = []
    for a, h, device in places:
        copy = line_copy(
            out_ref.at[device], full_ref.at[z * 8 + e], (plane_send, plane_recv), a * 2 + h,
            (device, z),
        )
        copy.start()
        plane.append(copy)
    full_ref[z * 8 + e] = out_ref[e]

    def inside(depth):
        return (depth >= 0) & (depth <= 3)

    def hop(line, sign, step, a):
        block = full_ref.at[pl.ds((z - sign * step) * 8 + pairs[a], 2)]
        return line_copy(block, block, line, step * 4 + a, (e, z + sign))

    def landed(line, sign, step, a):
        block = full_ref.at[pl.ds((z - sign * (step + 1)) * 8 + pairs[a], 2)]
        return line_copy(block, block, line, step * 4 + a, (e, z - sign))

    for step in range(4):
        for a in range(4):
            if step == 0:
                for copy, (chip, _, _) in zip(plane, places):
                    if chip == a:
                        copy.wait_recv()
            for line, sign in lines:
                if step > 0:

                    @pl.when(inside(z - sign * step))
                    def _(line=line, sign=sign, step=step, a=a):
                        landed(line, sign, step - 1, a).wait_recv()

                if step < 3:

                    @pl.when(inside(z - sign * step) & inside(z + sign))
                    def _(line=line, sign=sign, step=step, a=a):
                        hop(line, sign, step, a).start()

    for copy in plane:
        copy.wait_send()
    for step in range(3):
        for line, sign in lines:

            @pl.when(inside(z - sign * step) & inside(z + sign))
            def _(line=line, sign=sign, step=step):
                for a in range(4):
                    hop(line, sign, step, a).wait_send()


def return_kernel(
    part_ref, back_ref, leaving, arriving, result,
    plane_send, plane_recv, up_send, up_recv, down_send, down_recv,
):
    e, z, chips, places = plane_places()
    greet([(d, z) for _, _, d in places] + [(e, lax.rem(z + t, 4)) for t in (1, 2, 3)])
    lines = (((up_send, up_recv), 1), ((down_send, down_recv), -1))
    pairs = [lax.div(chip, 2) * 2 for chip in chips]

    def inside(depth):
        return (depth >= 0) & (depth <= 3)

    def hop(way, ahead, a):
        line, sign = lines[way]
        return line_copy(
            leaving.at[way, ahead - 1, a], arriving.at[way, ahead - 1, a], line,
            (ahead - 1) * 4 + a, (e, z + sign),
        )

    def landed(way, ahead, a):
        line, sign = lines[way]
        place = arriving.at[way, ahead, a]
        line_copy(place, place, line, ahead * 4 + a, (e, z - sign)).wait_recv()
        return place[...].astype(jnp.float32)

    def own(depth, a):
        return part_ref[pl.ds(depth * 8 + pairs[a], 2)]

    for ahead in (3, 2, 1):
        for a in (3, 1, 2, 0):
            for way, (_, sign) in enumerate(lines):

                @pl.when(inside(z + sign * ahead))
                def _(way=way, sign=sign, ahead=ahead, a=a):
                    leaving[way, ahead - 1, a] = own(z + sign * ahead, a)
                    if ahead < 3:

                        @pl.when(inside(z - sign))
                        def _():
                            value = own(z + sign * ahead, a).astype(jnp.float32)
                            value = value + landed(way, ahead, a)
                            leaving[way, ahead - 1, a] = value.astype(jnp.bfloat16)

                    hop(way, ahead, a).start()

    plane = []
    for a in (3, 1, 2, 0):
        result[a] = own(z, a).astype(jnp.float32)
        for way, (_, sign) in enumerate(lines):

            @pl.when(inside(z - sign))
            def _(way=way, a=a):
                result[a] = result[a] + landed(way, 0, a)

        for core in range(2):
            leaving[0, 3, a, core] = result[a, core].astype(jnp.bfloat16)
        for chip, h, device in places:
            if chip == a:
                copy = line_copy(
                    leaving.at[0, 3, a, lax.rem(device, 2)], back_ref.at[e],
                    (plane_send, plane_recv), a * 2 + h, (device, z),
                )
                copy.start()
                plane.append(copy)
    back_ref[e] = leaving[0, 3, 0, lax.rem(e, 2)]
    for copy in plane:
        copy.wait_recv()
    for copy in plane:
        copy.wait_send()
    for ahead in (3, 2, 1):
        for way, (_, sign) in enumerate(lines):

            @pl.when(inside(z + sign * ahead))
            def _(way=way, ahead=ahead):
                for a in range(4):
                    hop(way, ahead, a).wait_send()


def line_call(kernel, operand, blocks, scratch, number, name):
    _, rows, width = operand.shape
    vmem = pl.BlockSpec(memory_space=pltpu.VMEM)
    return pl.pallas_call(
        kernel,
        out_shape=jax.ShapeDtypeStruct((blocks, rows, width), operand.dtype),
        in_specs=[vmem],
        out_specs=vmem,
        scratch_shapes=scratch
        + [pltpu.SemaphoreType.DMA((8,))] * 2
        + [pltpu.SemaphoreType.DMA((12,))] * 4,
        compiler_params=pltpu.CompilerParams(
            collective_id=number, has_side_effects=True, vmem_limit_bytes=40 * 1024 * 1024
        ),
        cost_estimate=pl.CostEstimate(
            flops=0, bytes_accessed=80 * rows * width, transcendentals=0
        ),
        name=name,
    )(operand)


def dispatch_rows(outgoing):
    return line_call(dispatch_kernel, outgoing, 32, [], 2, "dispatch_rows")


def return_rows(partial):
    _, rows, width = partial.shape
    scratch = [
        pltpu.VMEM((2, 4, 4, 2, rows, width), partial.dtype),
        pltpu.VMEM((2, 3, 4, 2, rows, width), partial.dtype),
        pltpu.VMEM((4, 2, rows, width), jnp.float32),
    ]
    return line_call(return_kernel, partial, 8, scratch, 3, "return_rows")


def contract(left, right, left_axis, right_axis):
    return lax.dot_general(
        left, right, (((left_axis,), (right_axis,)), ((), ())), preferred_element_type=jnp.float32
    )


def attend_kernel(
    head_count, head_size, qkv_ref, column_ref, row_ref, offset_ref, out_ref, probs_ref
):
    rows = qkv_ref.shape[0]
    width = head_count * head_size
    allowed = column_ref[...] == row_ref[...]
    for pair in range(0, head_count, 2):
        halves = []
        for h in (pair, pair + 1):
            queries, keys, values = (
                qkv_ref[:, part * width + h * head_size : part * width + (h + 1) * head_size]
                for part in range(3)
            )
            bias = jnp.broadcast_to(offset_ref[h : h + 1, :], (rows, 2 * rows))
            bias = pltpu.roll(bias, 0, 1, stride=1, stride_axis=0)[:, :rows]
            scores = contract(queries, keys, 1, 1) * head_size ** (-0.5) + bias
            scores = jnp.where(allowed, scores, -1e30)
            weights = jnp.exp(scores - jnp.max(scores, axis=-1, keepdims=True))
            probs = weights / jnp.sum(weights, axis=-1, keepdims=True)
            probs_ref[h] = probs
            halves.append(contract(probs.astype(jnp.bfloat16), values, 1, 0))
        out_ref[:, pair * head_size : (pair + 2) * head_size] = jnp.concatenate(
            halves, axis=1
        ).astype(jnp.bfloat16)


def attend_back_kernel(
    head_count, head_size, qkv_ref, probs_ref, grad_ref, flip_ref, out_ref, offset_ref
):
    rows = qkv_ref.shape[0]
    width = head_count * head_size
    scale = head_size ** (-0.5)
    line = lax.broadcasted_iota(jnp.int32, (rows, rows), 0)
    lane = lax.broadcasted_iota(jnp.int32, (rows, rows), 1)
    for pair in range(0, head_count, 2):
        halves = []
        for h in (pair, pair + 1):
            queries, keys, values = (
                qkv_ref[:, part * width + h * head_size : part * width + (h + 1) * head_size]
                for part in range(3)
            )
            grad = grad_ref[:, h * head_size : (h + 1) * head_size]
            probs = probs_ref[h]
            grad_probs = contract(grad, values, 1, 1)
            inner = jnp.sum(probs * grad_probs, axis=-1, keepdims=True)
            scores = (probs * (grad_probs - inner)).astype(jnp.bfloat16)
            halves.append(
                (
                    contract(scores, keys, 1, 0) * scale,
                    contract(scores, queries, 0, 0) * scale,
                    contract(probs.astype(jnp.bfloat16), grad, 0, 0),
                )
            )
            turned = pltpu.roll(contract(flip_ref[...], scores, 1, 0), 1, 1, stride=1, stride_axis=0)
            ahead = jnp.where(lane <= line, turned, 0.0)
            offset_ref[h : h + 1, :rows] = jnp.sum(ahead, axis=0, keepdims=True)
            offset_ref[h : h + 1, rows:] = jnp.sum(turned - ahead, axis=0, keepdims=True)
        for part in range(3):
            start = part * width + pair * head_size
            out_ref[:, start : start + 2 * head_size] = jnp.concatenate(
                [halves[0][part], halves[1][part]], axis=1
            ).astype(jnp.bfloat16)


def attention_call(kernel, shapes, operands, name):
    vmem = pl.BlockSpec(memory_space=pltpu.VMEM)
    return pl.pallas_call(
        kernel,
        out_shape=shapes,
        in_specs=[vmem] * len(operands),
        out_specs=tuple(vmem for _ in shapes),
        compiler_params=pltpu.CompilerParams(vmem_limit_bytes=32 * 1024 * 1024),
        name=name,
    )(*operands)


def local(
    hidden_in,
    cotangent,
    lengths,
    routes,
    gain_attn,
    attn_qkv,
    attn_out,
    rel_bias,
    gain_ffn,
    router,
    expert_in,
    expert_out,
):
    row_count, model_width = hidden_in.shape
    bucket_count, head_count = rel_bias.shape
    head_size = model_width // head_count
    expert_count = router.shape[1]
    group_count = lax.axis_size("exp")
    local_count = expert_in.shape[0]
    capacity = max(2, row_count * 5 // (4 * expert_count))
    dp_count = lax.axis_size("dp")
    shard_rows = attn_qkv.shape[0]
    direct = group_count == 8 and dp_count == 4 and shard_rows % 8 == 0
    dense_width = 4 * model_width + expert_count
    full_width = -(-dense_width // lane_count) * lane_count
    shard = jnp.concatenate(
        [
            attn_qkv,
            attn_out,
            router,
            jnp.zeros((shard_rows, full_width - dense_width), jnp.bfloat16),
        ],
        axis=1,
    )
    if direct:
        full = gather_rows(shard)
    else:
        full = lax.all_gather(shard, ("exp", "dp"), axis=0, tiled=True)
    full_qkv = full[:, : 3 * model_width]
    full_out = full[:, 3 * model_width : 4 * model_width]
    full_route = full[:, 4 * model_width : dense_width]
    inputs = hidden_in.astype(jnp.float32)
    normed, attn_norm_pull = jax.vjp(rms_norm, inputs, gain_attn)
    normed_low = normed.astype(jnp.bfloat16)
    qkv_low = jnp.dot(normed_low, full_qkv, preferred_element_type=jnp.float32).astype(jnp.bfloat16)
    offset_table = bucket_table(row_count, bucket_count)
    offset_bucket = np.concatenate([offset_table[0], offset_table[:, 0][:1], offset_table[:0:-1, 0]])
    bucket_hot = jnp.asarray(
        offset_bucket[:, None] == np.arange(bucket_count)[None, :], dtype=jnp.float32
    )
    offset_bias = jnp.einsum("nb,bh->hn", bucket_hot, rel_bias, precision=lax.Precision.HIGHEST)
    segment = segment_ids(lengths, row_count)[0]
    attended_low, attn_probs = attention_call(
        functools.partial(attend_kernel, head_count, head_size),
        (
            jax.ShapeDtypeStruct((row_count, model_width), jnp.bfloat16),
            jax.ShapeDtypeStruct((head_count, row_count, row_count), jnp.float32),
        ),
        (qkv_low, segment[:, None], segment[None, :], offset_bias),
        "attend",
    )
    middle = inputs + jnp.dot(attended_low, full_out, preferred_element_type=jnp.float32)
    ffn_norm, ffn_norm_pull = jax.vjp(rms_norm, middle, gain_ffn)
    ffn_low = ffn_norm.astype(jnp.bfloat16)
    gate_probs = jax.nn.softmax(
        jnp.dot(ffn_low, full_route, preferred_element_type=jnp.float32), axis=-1
    )
    choose = routes == jnp.arange(expert_count, dtype=jnp.int32)[None, :]
    gate_prob = jnp.sum(jnp.where(choose, gate_probs, 0.0), axis=1, keepdims=True)
    earlier = jnp.asarray(np.tril(np.ones((row_count, row_count)), -1), dtype=jnp.bfloat16)
    rank_index = jnp.dot(earlier, choose.astype(jnp.bfloat16), preferred_element_type=jnp.float32)
    slot_index = jnp.sum(jnp.where(choose, rank_index, 0.0), axis=1).astype(jnp.int32)
    half_rows = local_count * capacity
    group_place = routes[:, 0] // local_count * half_rows
    slot_place = routes[:, 0] * capacity + slot_index + group_place
    dispatch = (
        jnp.arange(2 * group_count * half_rows, dtype=jnp.int32)[:, None]
        == jnp.concatenate([slot_place, slot_place + half_rows])[None, :]
    ).astype(jnp.bfloat16)
    grad_out = cotangent.astype(jnp.float32)
    grad_picked = (gate_prob * grad_out).astype(jnp.bfloat16)
    outgoing = jnp.dot(
        dispatch,
        jnp.concatenate([ffn_low, grad_picked], axis=0),
        preferred_element_type=jnp.float32,
    ).astype(jnp.bfloat16)
    outgoing = outgoing.reshape(group_count, 2 * half_rows, model_width)
    if direct:
        gathered = dispatch_rows(outgoing)
    else:
        arrived = lax.all_to_all(outgoing, "exp", split_axis=0, concat_axis=0, tiled=True)
        gathered = lax.all_gather(arrived, "dp", axis=0, tiled=True)
    slot_rows = dp_count * group_count * capacity
    gathered = gathered.reshape(-1, 2, local_count, capacity, model_width)
    gathered = jnp.transpose(gathered, (1, 2, 0, 3, 4)).reshape(
        2, local_count, slot_rows, model_width
    )
    expert_rows = gathered[0]
    grad_result = gathered[1]
    hidden_pre = jnp.einsum(
        "lsd,ldf->lsf", expert_rows, expert_in, preferred_element_type=jnp.float32
    )
    active_f32, gelu_pull = jax.vjp(gelu_tanh, hidden_pre)
    active = active_f32.astype(jnp.bfloat16)
    partial_out = jnp.einsum("lsf,lfd->lsd", active, expert_out, preferred_element_type=jnp.float32)
    grad_active = jnp.einsum(
        "lsd,lfd->lsf", grad_result, expert_out, preferred_element_type=jnp.float32
    )
    grad_pre = gelu_pull(grad_active)[0].astype(jnp.bfloat16)
    grad_part = jnp.einsum("lsf,ldf->lsd", grad_pre, expert_in, preferred_element_type=jnp.float32)
    grad_expert_out = jnp.einsum(
        "lsf,lsd->lfd", active, grad_result, preferred_element_type=jnp.float32
    )
    grad_expert_in = jnp.einsum(
        "lsd,lsf->ldf", expert_rows, grad_pre, preferred_element_type=jnp.float32
    )
    partial = jnp.stack(
        [partial_out.astype(jnp.bfloat16), grad_part.astype(jnp.bfloat16)]
    ).reshape(2, local_count, dp_count * group_count, capacity, model_width)
    partial = jnp.transpose(partial, (2, 0, 1, 3, 4)).reshape(-1, 2 * half_rows, model_width)
    if direct:
        returned = return_rows(partial)
    else:
        result_rows = lax.psum_scatter(partial, "dp", scatter_dimension=0, tiled=True)
        returned = lax.all_to_all(result_rows, "exp", split_axis=0, concat_axis=0, tiled=True)
    picked_both = lax.dot_general(
        dispatch,
        returned.reshape(-1, model_width),
        (((0,), (0,)), ((), ())),
        preferred_element_type=jnp.float32,
    )
    picked = picked_both[:row_count]
    grad_ffn = picked_both[row_count:]
    mixed = (middle + gate_prob * picked).astype(jnp.bfloat16)
    gate_grad = jnp.sum(grad_out * picked, axis=1, keepdims=True)
    logit_grad = (gate_probs * (jnp.where(choose, gate_grad, 0.0) - gate_prob * gate_grad)).astype(
        jnp.bfloat16
    )
    grad_ffn = grad_ffn + jnp.dot(logit_grad, full_route.T, preferred_element_type=jnp.float32)
    grad_middle_norm, grad_gain_ffn = ffn_norm_pull(grad_ffn)
    grad_middle = grad_out + grad_middle_norm
    branch_grad = grad_middle.astype(jnp.bfloat16)
    grad_attended = jnp.dot(branch_grad, full_out.T, preferred_element_type=jnp.float32).astype(
        jnp.bfloat16
    )
    grad_qkv, offset_grad = attention_call(
        functools.partial(attend_back_kernel, head_count, head_size),
        (
            jax.ShapeDtypeStruct((row_count, 3 * model_width), jnp.bfloat16),
            jax.ShapeDtypeStruct((head_count, 2 * row_count), jnp.float32),
        ),
        (
            qkv_low,
            attn_probs,
            grad_attended,
            jnp.asarray(np.eye(row_count)[::-1], dtype=jnp.bfloat16),
        ),
        "attend_back",
    )
    grad_bias = jnp.einsum("nb,hn->bh", bucket_hot, offset_grad, precision=lax.Precision.HIGHEST)
    grad_normed = jnp.dot(grad_qkv, full_qkv.T, preferred_element_type=jnp.float32)
    grad_inputs_norm, grad_gain_attn = attn_norm_pull(grad_normed)
    grad_in = grad_middle + grad_inputs_norm
    padded_logit = jnp.pad(logit_grad, ((0, 0), (0, full_width - dense_width)))
    dense_pairs = ((normed_low, grad_qkv), (attended_low, branch_grad), (ffn_low, padded_logit))
    if direct:
        small = jnp.concatenate([grad_gain_attn, grad_gain_ffn, grad_bias.reshape(-1)])
        small_size = small.shape[0]
        small_rows = -(-small_size // (8 * lane_count)) * 8
        small = jnp.pad(small, (0, small_rows * lane_count - small_size))
        owned, small = reduce_rows(
            [left.T for left, _ in dense_pairs] + [right for _, right in dense_pairs],
            shard_rows,
            small.reshape(small_rows, lane_count),
        )
        small = small.reshape(-1)
        grad_gain_attn = small[:model_width]
        grad_gain_ffn = small[model_width : 2 * model_width]
        grad_bias = small[2 * model_width : small_size].reshape(bucket_count, head_count)
    else:
        stacked = jnp.concatenate(
            [
                jnp.einsum("td,te->de", left, right, preferred_element_type=jnp.float32).astype(
                    jnp.bfloat16
                )
                for left, right in dense_pairs
            ],
            axis=1,
        )
        pieces = lax.all_to_all(
            stacked.reshape(group_count, dp_count * shard_rows, full_width),
            "exp",
            split_axis=0,
            concat_axis=0,
            tiled=True,
        ).astype(jnp.float32)
        pieces = jnp.sum(pieces, axis=0).reshape(dp_count, shard_rows, full_width)
        pieces = lax.all_to_all(
            pieces.astype(jnp.bfloat16), "dp", split_axis=0, concat_axis=0, tiled=True
        ).astype(jnp.float32)
        owned = jnp.sum(pieces, axis=0)
        grad_gain_attn, grad_gain_ffn, grad_bias = lax.psum(
            (grad_gain_attn, grad_gain_ffn, grad_bias), ("exp", "dp")
        )
    grad_attn_qkv = owned[:, : 3 * model_width]
    grad_attn_out = owned[:, 3 * model_width : 4 * model_width]
    grad_router = owned[:, 4 * model_width : dense_width]
    return (
        mixed,
        grad_in,
        grad_gain_attn,
        grad_attn_qkv,
        grad_attn_out,
        grad_bias,
        grad_gain_ffn,
        grad_router,
        grad_expert_in,
        grad_expert_out,
    )


def solution(mesh):
    return jax.shard_map(
        local,
        mesh=mesh,
        in_specs=(
            P(("exp", "dp"), None),
            P(("exp", "dp"), None),
            P(("exp", "dp"), None),
            P(("exp", "dp"), None),
            P(),
            P(("exp", "dp"), None),
            P(("exp", "dp"), None),
            P(),
            P(),
            P(("exp", "dp"), None),
            P("exp", None, "dp"),
            P("exp", "dp", None),
        ),
        out_specs=(
            P(("exp", "dp"), None),
            P(("exp", "dp"), None),
            P(),
            P(("exp", "dp"), None),
            P(("exp", "dp"), None),
            P(),
            P(),
            P(("exp", "dp"), None),
            P("exp", None, "dp"),
            P("exp", "dp", None),
        ),
        check_vma=False,
    )
```

```python
import functools

import jax
import jax.numpy as jnp
import numpy as np
from jax import lax
from jax.experimental import pallas as pl
from jax.experimental.pallas import tpu as pltpu
from jax.sharding import PartitionSpec as P

MESH = pl.DeviceIdType.MESH
lane_count = 128
by_y = (0, 3)

epsilon = 1e-06


def bucket_table(row_count, bucket_count):
    offset = np.arange(row_count)[None, :] - np.arange(row_count)[:, None]
    half_count = bucket_count // 2
    exact_count = half_count // 2
    spread = np.abs(offset)
    scaled = (
        np.log(np.maximum(spread, 1) / exact_count)
        / np.log(128.0 / exact_count)
        * (half_count - exact_count)
    )
    distant = np.minimum(exact_count + np.maximum(scaled, 0.0).astype(np.int32), half_count - 1)
    return ((offset > 0) * half_count + np.where(spread < exact_count, spread, distant)).astype(
        np.int32
    )


def rms_norm(values, gain_vec):
    return (
        values * lax.rsqrt(jnp.mean(values * values, axis=-1, keepdims=True) + epsilon) * gain_vec
    )


def gelu_tanh(values):
    return jax.nn.gelu(values, approximate=True)


def segment_ids(lengths, row_count):
    boundary = jnp.cumsum(lengths, axis=-1)
    position = jnp.arange(row_count, dtype=jnp.int32)
    return jnp.sum((position[:, None] >= boundary[..., None, :]).astype(jnp.int32), axis=-1)


def positions():
    e, z = lax.axis_index("exp"), lax.axis_index("dp")
    core, side_x, side_y = lax.rem(e, 2), lax.rem(lax.div(e, 2), 2), lax.div(e, 4)
    step_core, step_x, step_y = 1 - 2 * core, 2 - 4 * side_x, 4 - 8 * side_y
    chips = (e, e + step_x, e + step_y, e + step_x + step_y)
    return e, z, step_core, chips


def greet(devices):
    barrier = pltpu.get_barrier_semaphore()
    for device in devices:
        pl.semaphore_signal(barrier, inc=1, device_id=device, device_id_type=MESH)
    pl.semaphore_wait(barrier, len(devices))


def gather_kernel(mine_ref, full_ref, local_sem, send_sem, recv_sem):
    e, z, step_core, chips = positions()
    zs = [lax.rem(z + j, 4) for j in range(4)]
    partner = (e + step_core, z)
    beside = {1: (chips[1], z), 2: (chips[2], z)}
    along = {j: (e, zs[j]) for j in (1, 2, 3)}
    greet([partner, beside[1], beside[2], along[1], along[2], along[3]])
    sends = []

    def send(src, chip, j, device, recv):
        copy = pltpu.make_async_remote_copy(
            src_ref=src,
            dst_ref=full_ref.at[chips[chip] * 4 + zs[j]],
            send_sem=send_sem.at[len(sends)],
            recv_sem=recv_sem.at[recv],
            device_id=device,
            device_id_type=MESH,
        )
        copy.start()
        sends.append(copy)

    def held(chip, j):
        return full_ref.at[chips[chip] * 4 + zs[j]]

    def arrive(place, recv):
        pltpu.make_async_remote_copy(
            src_ref=place,
            dst_ref=place,
            send_sem=send_sem.at[0],
            recv_sem=recv_sem.at[recv],
            device_id=partner,
            device_id_type=MESH,
        ).wait_recv()

    def spread(src, j):
        send(src, 0, j, beside[1], 4 + j)
        send(src, 0, j, beside[2], 8 + j)
        send(src, 0, j, partner, 16 + j)

    def from_x(j):
        arrive(held(1, j), 4 + j)
        if j in by_y:
            send(held(1, j), 1, j, beside[2], 12 + j)
        send(held(1, j), 1, j, partner, 20 + j)

    def from_y(j):
        arrive(held(2, j), 8 + j)
        if j not in by_y:
            send(held(2, j), 2, j, beside[1], 12 + j)
        send(held(2, j), 2, j, partner, 24 + j)

    own = pltpu.make_async_copy(mine_ref, held(0, 0), local_sem)
    own.start()
    for j in (1, 3, 2):
        send(mine_ref, 0, 0, along[j], (4 - j) % 4)
    spread(mine_ref, 0)
    for j in (3, 1):
        arrive(held(0, j), j)
        spread(held(0, j), j)
    from_x(0)
    from_y(0)
    arrive(held(0, 2), 2)
    spread(held(0, 2), 2)
    for j in (3, 1, 2):
        from_x(j)
        from_y(j)
    for j in (0, 3, 1, 2):
        arrive(held(3, j), 12 + j)
        send(held(3, j), 3, j, partner, 28 + j)
    for chip in range(4):
        for j in range(4):
            arrive(full_ref.at[(chips[chip] + step_core) * 4 + zs[j]], 16 + chip * 4 + j)
    for copy in sends:
        copy.wait_send()
    own.wait()


def gather_rows(mine):
    rows, width = mine.shape
    full = pl.pallas_call(
        gather_kernel,
        out_shape=jax.ShapeDtypeStruct((32, rows, width), mine.dtype),
        in_specs=[pl.BlockSpec(memory_space=pl.ANY)],
        out_specs=pl.BlockSpec(memory_space=pl.ANY),
        scratch_shapes=[
            pltpu.SemaphoreType.DMA,
            pltpu.SemaphoreType.DMA((31,)),
            pltpu.SemaphoreType.DMA((32,)),
        ],
        compiler_params=pltpu.CompilerParams(collective_id=0, has_side_effects=True),
        cost_estimate=pl.CostEstimate(flops=0, bytes_accessed=64 * rows * width, transcendentals=0),
        name="gather_rows",
    )(mine)
    return full.reshape(32 * rows, width)


def reduce_kernel(
    normed_ref, attended_ref, ffn_ref, qkv_ref, branch_ref, logit_ref, small_ref,
    out_qkv_ref, out_out_ref, out_route_ref, total_ref,
    grad_ref, from_core, summed, passing, from_x, from_y, from_z,
    small_sum, small_in, small_z, send_sem, recv_sem, small_send, small_recv,
):
    e, z, step_core, chips = positions()
    zs = [lax.rem(z + j, 4) for j in range(4)]
    partner = (e + step_core, z)
    beside = {1: (chips[1], z), 2: (chips[2], z)}
    along = {j: (e, zs[j]) for j in (1, 2, 3)}
    greet([partner, beside[1], beside[2], along[1], along[2], along[3]])
    sends = []

    def send(src, dst, device, recv):
        copy = pltpu.make_async_remote_copy(
            src_ref=src,
            dst_ref=dst,
            send_sem=send_sem.at[len(sends)],
            recv_sem=recv_sem.at[recv],
            device_id=device,
            device_id_type=MESH,
        )
        copy.start()
        sends.append(copy)

    def small_copy(src, dst, device, number, recv):
        return pltpu.make_async_remote_copy(
            src_ref=src,
            dst_ref=dst,
            send_sem=small_send.at[number],
            recv_sem=small_recv.at[recv],
            device_id=device,
            device_id_type=MESH,
        )

    def arrive(place, recv):
        pltpu.make_async_remote_copy(
            src_ref=place,
            dst_ref=place,
            send_sem=send_sem.at[0],
            recv_sem=recv_sem.at[recv],
            device_id=partner,
            device_id_type=MESH,
        ).wait_recv()
        return place[...].astype(jnp.float32)

    def pair(chip, j):
        number = chip * 4 + j
        mine = grad_ref[chips[chip] * 4 + zs[j]].astype(jnp.float32)
        return mine + arrive(from_core.at[number], number)

    def step_sum(number, device):
        copy = small_copy(small_sum.at[number], small_in.at[number], device, number, number)
        copy.start()
        copy.wait_recv()
        small_sum[number + 1] = small_sum[number] + small_in[number]
        return copy

    def make(chip):
        count = normed_ref.shape[0] // 4
        group = lax.div(chips[chip], 2)
        here = pl.ds(pl.multiple_of(group * count, count), count)
        column = 0
        for left, right in ((normed_ref, qkv_ref), (attended_ref, branch_ref), (ffn_ref, logit_ref)):
            width = right.shape[1]
            step = width if width <= 768 else 768
            for start in range(0, width, step):
                part = jnp.dot(
                    left[here, :], right[:, start : start + step],
                    preferred_element_type=jnp.float32,
                )
                part = part.reshape(8, count // 8, step).astype(jnp.bfloat16)
                grad_ref[pl.ds(group * 8, 8), :, column + start : column + start + step] = part
            column += width

    def diagonal(j):
        number = 12 + j
        summed[number] = pair(3, j).astype(jnp.bfloat16)
        device = beside[2] if j in by_y else beside[1]
        send(summed.at[number], passing.at[j], device, 16 + j)

    def beside_chips(j):
        for chip in (2, 1) if j in by_y else (1, 2):
            number = chip * 4 + j
            value = pair(chip, j)
            if (j in by_y) == (chip == 1):
                value = value + arrive(passing.at[j], 16 + j)
            summed[number] = value.astype(jnp.bfloat16)
            landing = from_x if chip == 1 else from_y
            send(summed.at[number], landing.at[j], beside[chip], 16 + number)

    def own_chip(j):
        value = pair(0, j) + arrive(from_x.at[j], 20 + j) + arrive(from_y.at[j], 24 + j)
        if j == 0:
            for other in (1, 2, 3):
                value = value + arrive(from_z.at[other - 1], 27 + other)
            column = 0
            for owned_ref in (out_qkv_ref, out_out_ref, out_route_ref):
                owned_ref[...] = value[:, column : column + owned_ref.shape[1]]
                column += owned_ref.shape[1]
        else:
            summed[j] = value.astype(jnp.bfloat16)
            send(summed.at[j], from_z.at[3 - j], along[j], 31 - j)

    order = (2, 1, 3, 0)
    small_sum[0] = small_ref[...]
    for chip in (3, 1, 2, 0):
        make(chip)
        for j in order[:2]:
            place = (chips[chip] + step_core) * 4 + zs[j]
            send(grad_ref.at[place], from_core.at[chip * 4 + j], partner, chip * 4 + j)
    for j in order[2:]:
        for chip in (3, 1, 2, 0):
            place = (chips[chip] + step_core) * 4 + zs[j]
            send(grad_ref.at[place], from_core.at[chip * 4 + j], partner, chip * 4 + j)
    diagonal(order[0])
    diagonal(order[1])
    beside_chips(order[0])
    small_copies = [step_sum(0, partner)]
    diagonal(order[2])
    beside_chips(order[1])
    own_chip(order[0])
    small_copies.append(step_sum(1, beside[1]))
    diagonal(order[3])
    beside_chips(order[2])
    own_chip(order[1])
    small_copies.append(step_sum(2, beside[2]))
    beside_chips(order[3])
    small_z[0] = small_sum[3]
    for j in (1, 2, 3):
        copy = small_copy(small_z.at[0], small_z.at[4 - j], along[j], 2 + j, 6 - j)
        copy.start()
        small_copies.append(copy)
    own_chip(order[2])
    own_chip(order[3])
    for copy in small_copies[3:]:
        copy.wait_recv()
    spot = [lax.rem(4 + k - z, 4) for k in range(4)]
    total_ref[...] = (small_z[spot[0]] + small_z[spot[1]]) + (small_z[spot[2]] + small_z[spot[3]])
    for copy in sends + small_copies:
        copy.wait_send()


def reduce_rows(operands, rows, small):
    width = sum(right.shape[1] for right in operands[3:])
    vmem = pl.BlockSpec(memory_space=pltpu.VMEM)
    block = functools.partial(pltpu.VMEM, dtype=jnp.bfloat16)
    return pl.pallas_call(
        reduce_kernel,
        out_shape=tuple(
            jax.ShapeDtypeStruct((rows, right.shape[1]), jnp.float32) for right in operands[3:]
        )
        + (jax.ShapeDtypeStruct(small.shape, jnp.float32),),
        in_specs=[vmem] * 7,
        out_specs=(vmem,) * 4,
        scratch_shapes=[
            block((32, rows, width)),
            block((16, rows, width)),
            block((16, rows, width)),
            block((4, rows, width)),
            block((4, rows, width)),
            block((4, rows, width)),
            block((3, rows, width)),
            pltpu.VMEM((4,) + small.shape, jnp.float32),
            pltpu.VMEM((3,) + small.shape, jnp.float32),
            pltpu.VMEM((4,) + small.shape, jnp.float32),
            pltpu.SemaphoreType.DMA((31,)),
            pltpu.SemaphoreType.DMA((31,)),
            pltpu.SemaphoreType.DMA((6,)),
            pltpu.SemaphoreType.DMA((6,)),
        ],
        compiler_params=pltpu.CompilerParams(
            collective_id=1, has_side_effects=True, vmem_limit_bytes=40 * 1024 * 1024
        ),
        cost_estimate=pl.CostEstimate(
            flops=8192 * rows * width, bytes_accessed=4 * rows * width, transcendentals=0
        ),
        name="reduce_rows",
    )(*operands, small)


def line_copy(src, dst, sems, number, device):
    return pltpu.make_async_remote_copy(
        src_ref=src,
        dst_ref=dst,
        send_sem=sems[0].at[number],
        recv_sem=sems[1].at[number],
        device_id=device,
        device_id_type=MESH,
    )


def plane_places():
    e, z, step_core, chips = positions()
    places = [(a, h, chips[a] + h * step_core) for a in range(4) for h in range(2)]
    return e, z, chips, places[1:]


def dispatch_kernel(
    out_ref, full_ref, plane_send, plane_recv, up_send, up_recv, down_send, down_recv
):
    e, z, chips, places = plane_places()
    greet([(d, z) for _, _, d in places] + [(e, lax.rem(z + t, 4)) for t in (1, 2, 3)])
    lines = (((up_send, up_recv), 1), ((down_send, down_recv), -1))
    pairs = [lax.div(chip, 2) * 2 for chip in chips]
    plane = []
    for a, h, device in places:
        copy = line_copy(
            out_ref.at[device], full_ref.at[z * 8 + e], (plane_send, plane_recv), a * 2 + h,
            (device, z),
        )
        copy.start()
        plane.append(copy)
    full_ref[z * 8 + e] = out_ref[e]

    def inside(depth):
        return (depth >= 0) & (depth <= 3)

    def hop(line, sign, step, a):
        block = full_ref.at[pl.ds((z - sign * step) * 8 + pairs[a], 2)]
        return line_copy(block, block, line, step * 4 + a, (e, z + sign))

    def landed(line, sign, step, a):
        block = full_ref.at[pl.ds((z - sign * (step + 1)) * 8 + pairs[a], 2)]
        return line_copy(block, block, line, step * 4 + a, (e, z - sign))

    for step in range(4):
        for a in range(4):
            if step == 0:
                for copy, (chip, _, _) in zip(plane, places):
                    if chip == a:
                        copy.wait_recv()
            for line, sign in lines:
                if step > 0:

                    @pl.when(inside(z - sign * step))
                    def _(line=line, sign=sign, step=step, a=a):
                        landed(line, sign, step - 1, a).wait_recv()

                if step < 3:

                    @pl.when(inside(z - sign * step) & inside(z + sign))
                    def _(line=line, sign=sign, step=step, a=a):
                        hop(line, sign, step, a).start()

    for copy in plane:
        copy.wait_send()
    for step in range(3):
        for line, sign in lines:

            @pl.when(inside(z - sign * step) & inside(z + sign))
            def _(line=line, sign=sign, step=step):
                for a in range(4):
                    hop(line, sign, step, a).wait_send()


def return_kernel(
    part_ref, back_ref, leaving, arriving, result,
    plane_send, plane_recv, up_send, up_recv, down_send, down_recv,
):
    e, z, chips, places = plane_places()
    greet([(d, z) for _, _, d in places] + [(e, lax.rem(z + t, 4)) for t in (1, 2, 3)])
    lines = (((up_send, up_recv), 1), ((down_send, down_recv), -1))
    pairs = [lax.div(chip, 2) * 2 for chip in chips]

    def inside(depth):
        return (depth >= 0) & (depth <= 3)

    def hop(way, ahead, a):
        line, sign = lines[way]
        return line_copy(
            leaving.at[way, ahead - 1, a], arriving.at[way, ahead - 1, a], line,
            (ahead - 1) * 4 + a, (e, z + sign),
        )

    def landed(way, ahead, a):
        line, sign = lines[way]
        place = arriving.at[way, ahead, a]
        line_copy(place, place, line, ahead * 4 + a, (e, z - sign)).wait_recv()
        return place[...].astype(jnp.float32)

    def own(depth, a):
        return part_ref[pl.ds(depth * 8 + pairs[a], 2)]

    for ahead in (3, 2, 1):
        for a in (3, 1, 2, 0):
            for way, (_, sign) in enumerate(lines):

                @pl.when(inside(z + sign * ahead))
                def _(way=way, sign=sign, ahead=ahead, a=a):
                    leaving[way, ahead - 1, a] = own(z + sign * ahead, a)
                    if ahead < 3:

                        @pl.when(inside(z - sign))
                        def _():
                            value = own(z + sign * ahead, a).astype(jnp.float32)
                            value = value + landed(way, ahead, a)
                            leaving[way, ahead - 1, a] = value.astype(jnp.bfloat16)

                    hop(way, ahead, a).start()

    plane = []
    for a in (3, 1, 2, 0):
        result[a] = own(z, a).astype(jnp.float32)
        for way, (_, sign) in enumerate(lines):

            @pl.when(inside(z - sign))
            def _(way=way, a=a):
                result[a] = result[a] + landed(way, 0, a)

        for core in range(2):
            leaving[0, 3, a, core] = result[a, core].astype(jnp.bfloat16)
        for chip, h, device in places:
            if chip == a:
                copy = line_copy(
                    leaving.at[0, 3, a, lax.rem(device, 2)], back_ref.at[e],
                    (plane_send, plane_recv), a * 2 + h, (device, z),
                )
                copy.start()
                plane.append(copy)
    back_ref[e] = leaving[0, 3, 0, lax.rem(e, 2)]
    for copy in plane:
        copy.wait_recv()
    for copy in plane:
        copy.wait_send()
    for ahead in (3, 2, 1):
        for way, (_, sign) in enumerate(lines):

            @pl.when(inside(z + sign * ahead))
            def _(way=way, ahead=ahead):
                for a in range(4):
                    hop(way, ahead, a).wait_send()


def line_call(kernel, operand, blocks, scratch, number, name):
    _, rows, width = operand.shape
    vmem = pl.BlockSpec(memory_space=pltpu.VMEM)
    return pl.pallas_call(
        kernel,
        out_shape=jax.ShapeDtypeStruct((blocks, rows, width), operand.dtype),
        in_specs=[vmem],
        out_specs=vmem,
        scratch_shapes=scratch
        + [pltpu.SemaphoreType.DMA((8,))] * 2
        + [pltpu.SemaphoreType.DMA((12,))] * 4,
        compiler_params=pltpu.CompilerParams(
            collective_id=number, has_side_effects=True, vmem_limit_bytes=40 * 1024 * 1024
        ),
        cost_estimate=pl.CostEstimate(
            flops=0, bytes_accessed=80 * rows * width, transcendentals=0
        ),
        name=name,
    )(operand)


def dispatch_rows(outgoing):
    return line_call(dispatch_kernel, outgoing, 32, [], 2, "dispatch_rows")


def return_rows(partial):
    _, rows, width = partial.shape
    scratch = [
        pltpu.VMEM((2, 4, 4, 2, rows, width), partial.dtype),
        pltpu.VMEM((2, 3, 4, 2, rows, width), partial.dtype),
        pltpu.VMEM((4, 2, rows, width), jnp.float32),
    ]
    return line_call(return_kernel, partial, 8, scratch, 3, "return_rows")


def contract(left, right, left_axis, right_axis):
    return lax.dot_general(
        left, right, (((left_axis,), (right_axis,)), ((), ())), preferred_element_type=jnp.float32
    )


def attend_kernel(
    head_count, head_size, qkv_ref, column_ref, row_ref, offset_ref, out_ref, probs_ref
):
    rows = qkv_ref.shape[0]
    width = head_count * head_size
    allowed = column_ref[...] == row_ref[...]
    for pair in range(0, head_count, 2):
        halves = []
        for h in (pair, pair + 1):
            queries, keys, values = (
                qkv_ref[:, part * width + h * head_size : part * width + (h + 1) * head_size]
                for part in range(3)
            )
            bias = jnp.broadcast_to(offset_ref[h : h + 1, :], (rows, 2 * rows))
            bias = pltpu.roll(bias, 0, 1, stride=1, stride_axis=0)[:, :rows]
            scores = contract(queries, keys, 1, 1) * head_size ** (-0.5) + bias
            scores = jnp.where(allowed, scores, -1e30)
            weights = jnp.exp(scores - jnp.max(scores, axis=-1, keepdims=True))
            probs = weights / jnp.sum(weights, axis=-1, keepdims=True)
            probs_ref[h] = probs
            halves.append(contract(probs.astype(jnp.bfloat16), values, 1, 0))
        out_ref[:, pair * head_size : (pair + 2) * head_size] = jnp.concatenate(
            halves, axis=1
        ).astype(jnp.bfloat16)


def attend_back_kernel(
    head_count, head_size, qkv_ref, probs_ref, grad_ref, flip_ref, out_ref, offset_ref
):
    rows = qkv_ref.shape[0]
    width = head_count * head_size
    scale = head_size ** (-0.5)
    line = lax.broadcasted_iota(jnp.int32, (rows, rows), 0)
    lane = lax.broadcasted_iota(jnp.int32, (rows, rows), 1)
    for pair in range(0, head_count, 2):
        halves = []
        for h in (pair, pair + 1):
            queries, keys, values = (
                qkv_ref[:, part * width + h * head_size : part * width + (h + 1) * head_size]
                for part in range(3)
            )
            grad = grad_ref[:, h * head_size : (h + 1) * head_size]
            probs = probs_ref[h]
            grad_probs = contract(grad, values, 1, 1)
            inner = jnp.sum(probs * grad_probs, axis=-1, keepdims=True)
            scores = (probs * (grad_probs - inner)).astype(jnp.bfloat16)
            halves.append(
                (
                    contract(scores, keys, 1, 0) * scale,
                    contract(scores, queries, 0, 0) * scale,
                    contract(probs.astype(jnp.bfloat16), grad, 0, 0),
                )
            )
            turned = pltpu.roll(contract(flip_ref[...], scores, 1, 0), 1, 1, stride=1, stride_axis=0)
            ahead = jnp.where(lane <= line, turned, 0.0)
            offset_ref[h : h + 1, :rows] = jnp.sum(ahead, axis=0, keepdims=True)
            offset_ref[h : h + 1, rows:] = jnp.sum(turned - ahead, axis=0, keepdims=True)
        for part in range(3):
            start = part * width + pair * head_size
            out_ref[:, start : start + 2 * head_size] = jnp.concatenate(
                [halves[0][part], halves[1][part]], axis=1
            ).astype(jnp.bfloat16)


def attention_call(kernel, shapes, operands, name):
    vmem = pl.BlockSpec(memory_space=pltpu.VMEM)
    return pl.pallas_call(
        kernel,
        out_shape=shapes,
        in_specs=[vmem] * len(operands),
        out_specs=tuple(vmem for _ in shapes),
        compiler_params=pltpu.CompilerParams(vmem_limit_bytes=32 * 1024 * 1024),
        name=name,
    )(*operands)


def local(
    hidden_in,
    cotangent,
    lengths,
    routes,
    gain_attn,
    attn_qkv,
    attn_out,
    rel_bias,
    gain_ffn,
    router,
    expert_in,
    expert_out,
):
    row_count, model_width = hidden_in.shape
    bucket_count, head_count = rel_bias.shape
    head_size = model_width // head_count
    expert_count = router.shape[1]
    group_count = lax.axis_size("exp")
    local_count = expert_in.shape[0]
    capacity = max(2, row_count * 5 // (4 * expert_count))
    dp_count = lax.axis_size("dp")
    shard_rows = attn_qkv.shape[0]
    direct = group_count == 8 and dp_count == 4 and shard_rows % 8 == 0
    dense_width = 4 * model_width + expert_count
    full_width = -(-dense_width // lane_count) * lane_count
    shard = jnp.concatenate(
        [
            attn_qkv,
            attn_out,
            router,
            jnp.zeros((shard_rows, full_width - dense_width), jnp.bfloat16),
        ],
        axis=1,
    )
    if direct:
        full = gather_rows(shard)
    else:
        full = lax.all_gather(shard, ("exp", "dp"), axis=0, tiled=True)
    full_qkv = full[:, : 3 * model_width]
    full_out = full[:, 3 * model_width : 4 * model_width]
    full_route = full[:, 4 * model_width : dense_width]
    inputs = hidden_in.astype(jnp.float32)
    normed, attn_norm_pull = jax.vjp(rms_norm, inputs, gain_attn)
    normed_low = normed.astype(jnp.bfloat16)
    qkv_low = jnp.dot(normed_low, full_qkv, preferred_element_type=jnp.float32).astype(jnp.bfloat16)
    offset_table = bucket_table(row_count, bucket_count)
    offset_bucket = np.concatenate([offset_table[0], offset_table[:, 0][:1], offset_table[:0:-1, 0]])
    bucket_hot = jnp.asarray(
        offset_bucket[:, None] == np.arange(bucket_count)[None, :], dtype=jnp.float32
    )
    offset_bias = jnp.einsum("nb,bh->hn", bucket_hot, rel_bias, precision=lax.Precision.HIGHEST)
    segment = segment_ids(lengths, row_count)[0]
    attended_low, attn_probs = attention_call(
        functools.partial(attend_kernel, head_count, head_size),
        (
            jax.ShapeDtypeStruct((row_count, model_width), jnp.bfloat16),
            jax.ShapeDtypeStruct((head_count, row_count, row_count), jnp.float32),
        ),
        (qkv_low, segment[:, None], segment[None, :], offset_bias),
        "attend",
    )
    middle = inputs + jnp.dot(attended_low, full_out, preferred_element_type=jnp.float32)
    ffn_norm, ffn_norm_pull = jax.vjp(rms_norm, middle, gain_ffn)
    ffn_low = ffn_norm.astype(jnp.bfloat16)
    gate_probs = jax.nn.softmax(
        jnp.dot(ffn_low, full_route, preferred_element_type=jnp.float32), axis=-1
    )
    choose = routes == jnp.arange(expert_count, dtype=jnp.int32)[None, :]
    gate_prob = jnp.sum(jnp.where(choose, gate_probs, 0.0), axis=1, keepdims=True)
    earlier = jnp.asarray(np.tril(np.ones((row_count, row_count)), -1), dtype=jnp.bfloat16)
    rank_index = jnp.dot(earlier, choose.astype(jnp.bfloat16), preferred_element_type=jnp.float32)
    slot_index = jnp.sum(jnp.where(choose, rank_index, 0.0), axis=1).astype(jnp.int32)
    half_rows = local_count * capacity
    group_place = routes[:, 0] // local_count * half_rows
    slot_place = routes[:, 0] * capacity + slot_index + group_place
    dispatch = (
        jnp.arange(2 * group_count * half_rows, dtype=jnp.int32)[:, None]
        == jnp.concatenate([slot_place, slot_place + half_rows])[None, :]
    ).astype(jnp.bfloat16)
    grad_out = cotangent.astype(jnp.float32)
    grad_picked = (gate_prob * grad_out).astype(jnp.bfloat16)
    outgoing = jnp.dot(
        dispatch,
        jnp.concatenate([ffn_low, grad_picked], axis=0),
        preferred_element_type=jnp.float32,
    ).astype(jnp.bfloat16)
    outgoing = outgoing.reshape(group_count, 2 * half_rows, model_width)
    if direct:
        gathered = dispatch_rows(outgoing)
    else:
        arrived = lax.all_to_all(outgoing, "exp", split_axis=0, concat_axis=0, tiled=True)
        gathered = lax.all_gather(arrived, "dp", axis=0, tiled=True)
    slot_rows = dp_count * group_count * capacity
    gathered = gathered.reshape(-1, 2, local_count, capacity, model_width)
    gathered = jnp.transpose(gathered, (1, 2, 0, 3, 4)).reshape(
        2, local_count, slot_rows, model_width
    )
    expert_rows = gathered[0]
    grad_result = gathered[1]
    hidden_pre = jnp.einsum(
        "lsd,ldf->lsf", expert_rows, expert_in, preferred_element_type=jnp.float32
    )
    active_f32, gelu_pull = jax.vjp(gelu_tanh, hidden_pre)
    active = active_f32.astype(jnp.bfloat16)
    partial_out = jnp.einsum("lsf,lfd->lsd", active, expert_out, preferred_element_type=jnp.float32)
    grad_active = jnp.einsum(
        "lsd,lfd->lsf", grad_result, expert_out, preferred_element_type=jnp.float32
    )
    grad_pre = gelu_pull(grad_active)[0].astype(jnp.bfloat16)
    grad_part = jnp.einsum("lsf,ldf->lsd", grad_pre, expert_in, preferred_element_type=jnp.float32)
    grad_expert_out = jnp.einsum(
        "lsf,lsd->lfd", active, grad_result, preferred_element_type=jnp.float32
    )
    grad_expert_in = jnp.einsum(
        "lsd,lsf->ldf", expert_rows, grad_pre, preferred_element_type=jnp.float32
    )
    partial = jnp.stack(
        [partial_out.astype(jnp.bfloat16), grad_part.astype(jnp.bfloat16)]
    ).reshape(2, local_count, dp_count * group_count, capacity, model_width)
    partial = jnp.transpose(partial, (2, 0, 1, 3, 4)).reshape(-1, 2 * half_rows, model_width)
    if direct:
        returned = return_rows(partial)
    else:
        result_rows = lax.psum_scatter(partial, "dp", scatter_dimension=0, tiled=True)
        returned = lax.all_to_all(result_rows, "exp", split_axis=0, concat_axis=0, tiled=True)
    picked_both = lax.dot_general(
        dispatch,
        returned.reshape(-1, model_width),
        (((0,), (0,)), ((), ())),
        preferred_element_type=jnp.float32,
    )
    picked = picked_both[:row_count]
    grad_ffn = picked_both[row_count:]
    mixed = (middle + gate_prob * picked).astype(jnp.bfloat16)
    gate_grad = jnp.sum(grad_out * picked, axis=1, keepdims=True)
    logit_grad = (gate_probs * (jnp.where(choose, gate_grad, 0.0) - gate_prob * gate_grad)).astype(
        jnp.bfloat16
    )
    grad_ffn = grad_ffn + jnp.dot(logit_grad, full_route.T, preferred_element_type=jnp.float32)
    grad_middle_norm, grad_gain_ffn = ffn_norm_pull(grad_ffn)
    grad_middle = grad_out + grad_middle_norm
    branch_grad = grad_middle.astype(jnp.bfloat16)
    grad_attended = jnp.dot(branch_grad, full_out.T, preferred_element_type=jnp.float32).astype(
        jnp.bfloat16
    )
    grad_qkv, offset_grad = attention_call(
        functools.partial(attend_back_kernel, head_count, head_size),
        (
            jax.ShapeDtypeStruct((row_count, 3 * model_width), jnp.bfloat16),
            jax.ShapeDtypeStruct((head_count, 2 * row_count), jnp.float32),
        ),
        (
            qkv_low,
            attn_probs,
            grad_attended,
            jnp.asarray(np.eye(row_count)[::-1], dtype=jnp.bfloat16),
        ),
        "attend_back",
    )
    grad_bias = jnp.einsum("nb,hn->bh", bucket_hot, offset_grad, precision=lax.Precision.HIGHEST)
    grad_normed = jnp.dot(grad_qkv, full_qkv.T, preferred_element_type=jnp.float32)
    grad_inputs_norm, grad_gain_attn = attn_norm_pull(grad_normed)
    grad_in = grad_middle + grad_inputs_norm
    padded_logit = jnp.pad(logit_grad, ((0, 0), (0, full_width - dense_width)))
    dense_pairs = ((normed_low, grad_qkv), (attended_low, branch_grad), (ffn_low, padded_logit))
    if direct:
        small = jnp.concatenate([grad_gain_attn, grad_gain_ffn, grad_bias.reshape(-1)])
        small_size = small.shape[0]
        small_rows = -(-small_size // (8 * lane_count)) * 8
        small = jnp.pad(small, (0, small_rows * lane_count - small_size))
        grad_attn_qkv, grad_attn_out, grad_router, small = reduce_rows(
            [left.T for left, _ in dense_pairs] + [right for _, right in dense_pairs],
            shard_rows,
            small.reshape(small_rows, lane_count),
        )
        small = small.reshape(-1)
        grad_gain_attn = small[:model_width]
        grad_gain_ffn = small[model_width : 2 * model_width]
        grad_bias = small[2 * model_width : small_size].reshape(bucket_count, head_count)
    else:
        stacked = jnp.concatenate(
            [
                jnp.einsum("td,te->de", left, right, preferred_element_type=jnp.float32).astype(
                    jnp.bfloat16
                )
                for left, right in dense_pairs
            ],
            axis=1,
        )
        pieces = lax.all_to_all(
            stacked.reshape(group_count, dp_count * shard_rows, full_width),
            "exp",
            split_axis=0,
            concat_axis=0,
            tiled=True,
        ).astype(jnp.float32)
        pieces = jnp.sum(pieces, axis=0).reshape(dp_count, shard_rows, full_width)
        pieces = lax.all_to_all(
            pieces.astype(jnp.bfloat16), "dp", split_axis=0, concat_axis=0, tiled=True
        ).astype(jnp.float32)
        owned = jnp.sum(pieces, axis=0)
        grad_gain_attn, grad_gain_ffn, grad_bias = lax.psum(
            (grad_gain_attn, grad_gain_ffn, grad_bias), ("exp", "dp")
        )
        grad_attn_qkv = owned[:, : 3 * model_width]
        grad_attn_out = owned[:, 3 * model_width : 4 * model_width]
        grad_router = owned[:, 4 * model_width :]
    grad_router = grad_router[:, :expert_count]
    return (
        mixed,
        grad_in,
        grad_gain_attn,
        grad_attn_qkv,
        grad_attn_out,
        grad_bias,
        grad_gain_ffn,
        grad_router,
        grad_expert_in,
        grad_expert_out,
    )


def solution(mesh):
    return jax.shard_map(
        local,
        mesh=mesh,
        in_specs=(
            P(("exp", "dp"), None),
            P(("exp", "dp"), None),
            P(("exp", "dp"), None),
            P(("exp", "dp"), None),
            P(),
            P(("exp", "dp"), None),
            P(("exp", "dp"), None),
            P(),
            P(),
            P(("exp", "dp"), None),
            P("exp", None, "dp"),
            P("exp", "dp", None),
        ),
        out_specs=(
            P(("exp", "dp"), None),
            P(("exp", "dp"), None),
            P(),
            P(("exp", "dp"), None),
            P(("exp", "dp"), None),
            P(),
            P(),
            P(("exp", "dp"), None),
            P("exp", None, "dp"),
            P("exp", "dp", None),
        ),
        check_vma=False,
    )
```
